32 devices in a mesh: seq: 8 (over y, x, core), head: 4 (over z).
Axes of the slice: x: 2, y: 2, z: 4, core: 2. Of those that a mesh axis runs over, the one named last changes fastest.
Arguments:
- byte_states: bfloat16 [4, 1024, 1024], P('head', 'seq'), may hold values from -6 to 6
- log_decay: float32 [4, 1024, 32], P('head', 'seq'), may hold values from -2.5 to 0
- group_starts: int32 [4, 192], P('head'), may hold values from 0 to 1023, as said below
- in_weight: bfloat16 [1024, 4352], P('head'), may hold values from -0.1875 to 0.1875
- conv_weight: float32 [4, 2304], replicated, may hold values from -2.5 to 2.5
- norm_gain: float32 [2048], replicated, may hold values from 0.1 to 1.9
- out_weight: bfloat16 [2048, 1024], P('head'), may hold values from -0.125 to 0.125
- qkv_weight: bfloat16 [1024, 3, 4, 128], P(None, None, 'head'), may hold values from -1.5 to 1.5
Outputs:
- encoded: bfloat16 [4, 1024, 1024], P('head', 'seq')
- attended: bfloat16 [4, 192, 4, 128], P(None, 'seq', 'head')
The draws below stay inside these ranges and needn't reach their ends.
Inputs may be any that keep to these rules, and one draw needn't show every extreme that they name: `group_starts`: strictly increasing, the first entry 0; every group k has all its bytes on the indices k // 24 - 1 to k // 24 + 1 of seq, each index holding 128 consecutive bytes; between 12 and 36 groups begin within the bytes of one index of seq.
All inputs are finite; a program needn't handle non-finite values.
Results may differ from the reference program's by a relative error of at most 0.0095.
Values may be sent and summed in bfloat16 or wider, within the bound.
A program may use at most 128 MiB of HBM per device.

```python
import math
import jax
import jax.numpy as jnp
from jax import lax

D = 1024
SCAN_CHANNELS = 32
STATE = 128
CONV = 4
AHD = 128
BLOCK = 128
BYTES_DEV = 128
DI = 2048
AHEADS = 4
STRING_TOTAL = 4
OCTET_SPAN = 1024
GROUPS_DEV = 24
GROUPS = 192


def draw_log_decay(key, part):
    stochastic_seeds = jax.random.split(key, 7)
    slow_share = 0.5
    slow_heads = jax.random.uniform(stochastic_seeds[0], (STRING_TOTAL, 1, SCAN_CHANNELS)) < slow_share
    slow_rate = jnp.exp(jax.random.uniform(stochastic_seeds[1], (STRING_TOTAL, 1, SCAN_CHANNELS), minval=math.log(0.2), maxval=math.log(0.6))) / OCTET_SPAN
    fast_rate = jnp.exp(jax.random.uniform(stochastic_seeds[2], (STRING_TOTAL, 1, SCAN_CHANNELS), minval=math.log(1.0 / 50.0), maxval=math.log(1.0 / 30.0)))
    ambient_frequency = jnp.where(slow_heads, slow_rate, fast_rate)
    shard_total = OCTET_SPAN // BYTES_DEV
    processor_scaling = jnp.exp(jax.random.uniform(stochastic_seeds[3], (STRING_TOTAL, shard_total, 1, 1), minval=math.log(0.5), maxval=math.log(2.0)))
    processor_scaling = jnp.broadcast_to(processor_scaling, (STRING_TOTAL, shard_total, BYTES_DEV, 1)).reshape(STRING_TOTAL, OCTET_SPAN, 1)
    location_scaling = jax.random.uniform(stochastic_seeds[4], (STRING_TOTAL, OCTET_SPAN, SCAN_CHANNELS), minval=0.5, maxval=1.5)
    cluster_location = jax.random.randint(stochastic_seeds[5], (STRING_TOTAL, 1, 3), 0, OCTET_SPAN)
    cluster_extent = jax.random.uniform(stochastic_seeds[6], (STRING_TOTAL, 3, SCAN_CHANNELS), minval=0.22, maxval=0.69)
    agreement_tally = (jnp.arange(OCTET_SPAN, dtype=jnp.int32)[None, :, None] == cluster_location).astype(jnp.float32)
    cluster_catalog = jnp.einsum('ube,uei->ubi', agreement_tally, cluster_extent)
    return (-(ambient_frequency * processor_scaling * location_scaling + cluster_catalog)).astype(jnp.float32)


def draw_group_starts(key, part):
    shard_total = OCTET_SPAN // BYTES_DEV
    first_key, second_key = jax.random.split(key)
    offsets = jax.random.randint(first_key, (STRING_TOTAL, shard_total // 2), -(GROUPS_DEV // 2), GROUPS_DEV // 2 + 1)
    counts = jnp.stack([GROUPS_DEV - offsets, GROUPS_DEV + offsets], axis=-1).reshape(STRING_TOTAL, shard_total)
    within = jnp.arange(BYTES_DEV, dtype=jnp.int32)
    scores = jax.random.randint(second_key, (STRING_TOTAL, shard_total, BYTES_DEV), 0, 1 << 20) * BYTES_DEV + within
    leading = (jnp.arange(shard_total, dtype=jnp.int32)[None, :, None] == 0) & (within[None, None, :] == 0)
    scores = jnp.where(leading, -1, scores)
    ordering = jnp.argsort(scores, axis=-1, stable=True)
    rank_of = jnp.argsort(ordering, axis=-1, stable=True)
    chosen = rank_of < counts[:, :, None]
    chosen_flat = chosen.reshape(STRING_TOTAL, OCTET_SPAN)
    picked = jnp.argsort(jnp.where(chosen_flat, 0, 1), axis=-1, stable=True)[:, :GROUPS]
    return picked.astype(jnp.int32)


def draw_qkv_weight(key, part):
    stochastic_seeds = jax.random.split(key, 4)
    base_part = jax.random.normal(stochastic_seeds[0], (D, AHEADS, AHD), jnp.float32) / math.sqrt(D)
    values_part = jax.random.normal(stochastic_seeds[1], (D, AHEADS, AHD), jnp.float32) / math.sqrt(D)
    query_part = base_part
    key_part = jax.random.normal(stochastic_seeds[3], (D, AHEADS, AHD), jnp.float32) / math.sqrt(D)
    stacked = jnp.stack([query_part, key_part, values_part], axis=1)
    return jnp.clip(stacked, -1.5, 1.5).astype(jnp.bfloat16)


def block_levels(rng, dims, shards, low, largest):
    factor_of = 1.0
    for position, shards_of in shards:
        heights = jax.random.uniform(jax.random.fold_in(jax.random.fold_in(rng, 6), position), (shards_of,), jnp.float32, low / len(shards), largest / len(shards))
        factor_of = factor_of * jnp.repeat(jnp.exp(heights), dims[position] // shards_of).reshape((-1,) + (1,) * (len(dims) - 1 - position))
    return factor_of


def gaussian(rng, dims, deviation, most, pieces=(), kind=jnp.bfloat16):
    loudness = block_levels(rng, dims, pieces, -0.22, 0.18) if pieces else 1.0
    array = jax.random.normal(rng, dims, jnp.float32) * deviation * loudness
    return jnp.minimum(jnp.maximum(array, -most), most).astype(kind)


def setup_inputs(seed: int = 0) -> dict:
    streams_of = jax.random.split(jax.random.key(seed), 9)
    return {
        "byte_states": gaussian(streams_of[0], (STRING_TOTAL, OCTET_SPAN, D), 1.0, 6.0, ((0, 4), (1, 8))),
        "log_decay": draw_log_decay(jax.random.fold_in(streams_of[8], 71), 0),
        "group_starts": draw_group_starts(jax.random.fold_in(streams_of[8], 71), 0),
        "in_weight": gaussian(streams_of[3], (D, 2 * DI + 2 * STATE), D ** -0.5, 0.1875, ((0, 4),)),
        "conv_weight": gaussian(streams_of[4], (CONV, DI + 2 * STATE), 0.5, 2.5, (), jnp.float32),
        "norm_gain": jnp.clip(1.0 + 0.18 * jax.random.normal(streams_of[5], (DI,), jnp.float32), 0.1, 1.9),
        "out_weight": gaussian(streams_of[6], (DI, D), DI ** -0.5, 0.125, ((0, 4),)),
        "qkv_weight": draw_qkv_weight(jax.random.fold_in(streams_of[8], 71), 0),
    }


highest = lax.Precision.HIGHEST

def state_block(hidden_state, block_items):
    head_inputs, write_vectors, read_vectors, decays = block_items
    cumulative = jnp.cumsum(decays, axis=0)
    length = decays.shape[0]
    later_index = lax.broadcasted_iota(jnp.int32, (length, length), 0)
    earlier_index = lax.broadcasted_iota(jnp.int32, (length, length), 1)
    causal = (earlier_index <= later_index)[None]
    spread = cumulative.T[:, :, None] - cumulative.T[:, None, :]
    factor = jnp.where(causal, jnp.exp(jnp.where(causal, spread, 0.0)), 0.0)
    gram_matrix = jnp.dot(read_vectors, write_vectors.T, preferred_element_type=jnp.float32)
    mixed_gram = lax.optimization_barrier((factor * gram_matrix[None]).astype(jnp.bfloat16)).astype(jnp.float32)
    float_inputs = head_inputs.astype(jnp.float32)
    float_reads = read_vectors.astype(jnp.float32)
    float_writes = write_vectors.astype(jnp.float32)
    output = jnp.einsum('hts,shp->thp', mixed_gram, float_inputs, precision=highest)
    output = output + jnp.exp(cumulative)[:, :, None] * jnp.einsum('tn,hpn->thp', float_reads, hidden_state, precision=highest)
    final_log = cumulative[-1]
    tail_decay = jnp.exp(final_log[None, :] - cumulative)
    weighted = lax.optimization_barrier((float_inputs * tail_decay[:, :, None]).astype(jnp.bfloat16)).astype(jnp.float32)
    fresh_part = jnp.einsum('shp,sn->hpn', weighted, float_writes, precision=highest)
    hidden_state = jnp.exp(final_log)[:, None, None] * hidden_state + fresh_part
    return (hidden_state, output)

def convolve(padded, conv_weight, length):
    summed = jnp.zeros((length, padded.shape[1]), jnp.float32)
    for offset in range(conv_weight.shape[0]):
        summed = summed + conv_weight[offset] * padded[offset:offset + length].astype(jnp.float32)
    return jax.nn.silu(summed).astype(jnp.bfloat16)

def encode(states, decays, in_weight, conv_weight, norm_gain, out_weight):
    length = states.shape[0]
    head_count = decays.shape[1]
    inner_width = norm_gain.shape[0]
    head_dim = inner_width // head_count
    state_width = (in_weight.shape[1] - 2 * inner_width) // 2
    float_states = states.astype(jnp.float32)
    normed = (float_states * lax.rsqrt(lax.optimization_barrier(jnp.mean(float_states * float_states, axis=-1, keepdims=True)) + 1e-05)).astype(jnp.bfloat16)
    projected = jnp.dot(normed, in_weight, preferred_element_type=jnp.float32).astype(jnp.bfloat16)
    gate_part = projected[:, :inner_width]
    mixer_in = projected[:, inner_width:]
    tap_count = conv_weight.shape[0]
    padded = jnp.concatenate([jnp.zeros((tap_count - 1, mixer_in.shape[1]), jnp.bfloat16), mixer_in], axis=0)
    convolved = convolve(padded, conv_weight, length)
    head_inputs = convolved[:, :inner_width].reshape(length, head_count, head_dim)
    write_vectors = convolved[:, inner_width:inner_width + state_width]
    read_vectors = convolved[:, inner_width + state_width:]
    block_rows = BLOCK
    block_count = length // block_rows
    start_state = jnp.zeros((head_count, head_dim, state_width), jnp.float32)
    block_items = (head_inputs.reshape(block_count, block_rows, head_count, head_dim), write_vectors.reshape(block_count, block_rows, state_width), read_vectors.reshape(block_count, block_rows, state_width), decays.reshape(block_count, block_rows, head_count))
    final_state, outputs = lax.scan(state_block, start_state, block_items)
    outputs = outputs.reshape(length, head_count, head_dim)
    gated_out = outputs * jax.nn.silu(gate_part.astype(jnp.float32)).reshape(length, head_count, head_dim)
    scaled = gated_out * lax.rsqrt(lax.optimization_barrier(jnp.mean(gated_out * gated_out, axis=-1, keepdims=True)) + 1e-05) * norm_gain.reshape(head_count, head_dim)
    flat_heads = scaled.reshape(length, inner_width).astype(jnp.bfloat16)
    branch = jnp.dot(flat_heads, out_weight, preferred_element_type=jnp.float32)
    return (float_states + branch).astype(jnp.bfloat16)

def attend(encoded, starts, qkv_weight):
    length, model_width = encoded.shape
    groups = starts.shape[0]
    positions = jnp.arange(length, dtype=jnp.int32)
    group_id = (lax.optimization_barrier(jnp.sum((starts[None, :] <= positions[:, None]).astype(jnp.int32), axis=1)) - 1).astype(jnp.int32)
    pooled = jax.ops.segment_sum(encoded.astype(jnp.float32), group_id, num_segments=groups)
    normed = (pooled * lax.rsqrt(lax.optimization_barrier(jnp.mean(pooled * pooled, axis=-1, keepdims=True)) + 1e-05)).astype(jnp.bfloat16)
    head_count = qkv_weight.shape[2]
    key_width = qkv_weight.shape[3]
    triple = jnp.dot(normed, qkv_weight.reshape(model_width, 3 * head_count * key_width), preferred_element_type=jnp.float32)
    triple = triple.astype(jnp.bfloat16).reshape(groups, 3, head_count, key_width).astype(jnp.float32)
    query_rows = triple[:, 0]
    key_rows = triple[:, 1]
    values = triple[:, 2]
    scores = jnp.einsum('qhd,khd->hqk', query_rows, key_rows) / math.sqrt(key_width)
    query_index = lax.broadcasted_iota(jnp.int32, (groups, groups), 0)
    key_index = lax.broadcasted_iota(jnp.int32, (groups, groups), 1)
    allowed = (key_index <= query_index)[None]
    row_max = lax.optimization_barrier(jnp.max(jnp.where(allowed, scores, -1e+30), axis=-1, keepdims=True))
    exp_scores = jnp.where(allowed, jnp.exp(jnp.where(allowed, scores - row_max, 0.0)), 0.0)
    row_total = lax.optimization_barrier(jnp.sum(exp_scores, axis=-1))
    rounded = lax.optimization_barrier(exp_scores.astype(jnp.bfloat16)).astype(jnp.float32)
    summed = jnp.einsum('hqk,khd->qhd', rounded, values)
    return (summed / row_total.T[:, :, None]).astype(jnp.bfloat16)

def reference(byte_states, log_decay, group_starts, in_weight, conv_weight, norm_gain, out_weight, qkv_weight):

    def per_sequence(sequence_items):
        states, decays, starts = sequence_items
        encoded = encode(states, decays, in_weight, conv_weight, norm_gain, out_weight)
        return (encoded, attend(encoded, starts, qkv_weight))
    encoded, attended = lax.map(per_sequence, (byte_states, log_decay, group_starts))
    return (encoded, attended)
```

```python
import math

import jax
import jax.numpy as jnp
from jax import lax
from jax.sharding import PartitionSpec as P

BLOCK = 128


highest = lax.Precision.HIGHEST


def passed_along(value, axis, steps):
    count = lax.axis_size(axis)
    first, last = (max(0, -steps), min(count, count - steps))
    return lax.ppermute(value, axis, [(source, source + steps) for source in range(first, last)])


def entering(x, axis, combine, identity):
    length, place = (lax.axis_size(axis), lax.axis_index(axis))
    everything = jax.tree.map(
        lambda part, kind: lax.all_gather(part.astype(kind), axis), x, (jnp.bfloat16, jnp.bfloat16)
    )
    start = jax.tree.map(
        lambda part, zero: jnp.broadcast_to(jnp.asarray(zero, part.dtype), part.shape), x, identity
    )

    def lap(k, before):
        reached = k < place
        new = combine(
            before, jax.tree.map(lambda part, own: part[k].astype(own.dtype), everything, x)
        )
        return jax.tree.map(lambda a, b: jnp.where(reached, a, b), new, before)

    return lax.fori_loop(0, length, lap, start)


def running_sum(values):
    length = values.shape[0]
    row = lax.broadcasted_iota(jnp.int32, (length, length), 0)
    column = lax.broadcasted_iota(jnp.int32, (length, length), 1)
    return jnp.dot((column <= row).astype(jnp.float32), values, precision=highest)


def state_block(hidden_state, block_items):
    head_inputs, write_vectors, read_vectors, decays = block_items
    cumulative = running_sum(decays)
    length = decays.shape[0]
    later_index = lax.broadcasted_iota(jnp.int32, (length, length), 0)
    earlier_index = lax.broadcasted_iota(jnp.int32, (length, length), 1)
    causal = (earlier_index <= later_index)[None]
    spread = cumulative.T[:, :, None] - cumulative.T[:, None, :]
    factor = jnp.where(causal, jnp.exp(jnp.where(causal, spread, 0.0)), 0.0)
    gram_matrix = jnp.dot(read_vectors, write_vectors.T, preferred_element_type=jnp.float32)
    mixed_gram = (factor * gram_matrix[None]).astype(jnp.bfloat16)
    output = jnp.einsum("hts,shp->thp", mixed_gram, head_inputs, preferred_element_type=jnp.float32)
    float_reads = read_vectors.astype(jnp.float32)
    output = output + jnp.exp(cumulative)[:, :, None] * jnp.einsum(
        "tn,hpn->thp", float_reads, hidden_state, precision=highest
    )
    final_log = cumulative[-1]
    tail_decay = jnp.exp(final_log[None, :] - cumulative)
    weighted = (head_inputs.astype(jnp.float32) * tail_decay[:, :, None]).astype(jnp.bfloat16)
    fresh_part = jnp.einsum(
        "shp,sn->hpn", weighted, write_vectors, preferred_element_type=jnp.float32
    )
    hidden_state = jnp.exp(final_log)[:, None, None] * hidden_state + fresh_part
    return (hidden_state, output)


def convolve(padded, conv_weight, length):
    summed = jnp.zeros((length, padded.shape[1]), jnp.float32)
    for offset in range(conv_weight.shape[0]):
        summed = summed + conv_weight[offset] * padded[offset : offset + length].astype(jnp.float32)
    return jax.nn.silu(summed).astype(jnp.bfloat16)


def combine_states(earlier, later):
    return (earlier[0] + later[0], jnp.exp(later[0])[:, None, None] * earlier[1] + later[1])


def local(
    byte_states, log_decay, group_starts, in_weight, conv_weight, norm_gain, out_weight, qkv_weight
):
    states = byte_states[0]
    decays = log_decay[0]
    starts = group_starts[0]
    row_count = states.shape[0]
    model_width = states.shape[1]
    head_count = decays.shape[1]
    inner_width = norm_gain.shape[0]
    head_dim = inner_width // head_count
    state_width = (in_weight.shape[1] - 2 * inner_width) // 2
    float_states = states.astype(jnp.float32)
    normed = (
        float_states
        * lax.rsqrt(jnp.mean(float_states * float_states, axis=-1, keepdims=True) + 1e-05)
    ).astype(jnp.bfloat16)
    columns = normed
    projected = jnp.dot(
        columns,
        lax.all_gather(in_weight, "head", axis=0, tiled=True),
        preferred_element_type=jnp.float32,
    )
    projected = projected.astype(jnp.bfloat16)
    gate_part = projected[:, :inner_width]
    mixer_in = projected[:, inner_width:]
    tap_count = conv_weight.shape[0]
    left_rim = passed_along(mixer_in[row_count - (tap_count - 1) :], "seq", 1)
    padded = jnp.concatenate([left_rim, mixer_in], axis=0)
    convolved = convolve(padded, conv_weight, row_count)
    head_inputs = convolved[:, :inner_width].reshape(row_count, head_count, head_dim)
    write_vectors = convolved[:, inner_width : inner_width + state_width]
    read_vectors = convolved[:, inner_width + state_width :]
    block_rows = BLOCK
    block_count = row_count // block_rows
    start_state = jnp.zeros((head_count, head_dim, state_width), jnp.float32)
    block_items = (
        head_inputs.reshape(block_count, block_rows, head_count, head_dim),
        write_vectors.reshape(block_count, block_rows, state_width),
        read_vectors.reshape(block_count, block_rows, state_width),
        decays.reshape(block_count, block_rows, head_count),
    )
    local_state, outputs = lax.scan(state_block, start_state, block_items)
    outputs = outputs.reshape(row_count, head_count, head_dim)
    cumulative = running_sum(decays)
    identity = (jnp.zeros((head_count,), jnp.float32), jnp.zeros_like(local_state))
    carried = entering((cumulative[-1], local_state), "seq", combine_states, identity)
    outputs = outputs + jnp.exp(cumulative)[:, :, None] * jnp.einsum(
        "tn,hpn->thp", read_vectors.astype(jnp.float32), carried[1], precision=highest
    )
    gated_out = outputs * jax.nn.silu(gate_part.astype(jnp.float32)).reshape(
        row_count, head_count, head_dim
    )
    scaled = (
        gated_out
        * lax.rsqrt(jnp.mean(gated_out * gated_out, axis=-1, keepdims=True) + 1e-05)
        * norm_gain.reshape(head_count, head_dim)
    )
    flat_heads = scaled.reshape(row_count, inner_width).astype(jnp.bfloat16)
    columns = flat_heads
    branch = jnp.dot(
        columns,
        lax.all_gather(out_weight, "head", axis=0, tiled=True),
        preferred_element_type=jnp.float32,
    )
    encoded = (float_states + branch).astype(jnp.bfloat16)
    seq_count = lax.axis_size("seq")
    seq_index = lax.axis_index("seq")
    groups = starts.shape[0]
    per_device = groups // seq_count
    positions = seq_index * row_count + jnp.arange(row_count, dtype=jnp.int32)
    group_id = jnp.sum((starts[None, :] <= positions[:, None]).astype(jnp.int32), axis=1) - 1
    contract_rows = (((0,), (0,)), ((), ()))
    local_id = group_id - (seq_index - 1) * per_device
    onehot = (local_id[:, None] == jnp.arange(3 * per_device, dtype=jnp.int32)[None, :]).astype(
        jnp.bfloat16
    )
    partial_value = lax.dot_general(
        onehot, encoded, contract_rows, preferred_element_type=jnp.float32
    )
    from_above = passed_along(partial_value[:per_device].astype(jnp.bfloat16), "seq", -1).astype(
        jnp.float32
    )
    from_below = passed_along(
        partial_value[2 * per_device :].astype(jnp.bfloat16), "seq", 1
    ).astype(jnp.float32)
    pooled = partial_value[per_device : 2 * per_device] + from_above + from_below
    group_normed = (
        pooled * lax.rsqrt(jnp.mean(pooled * pooled, axis=-1, keepdims=True) + 1e-05)
    ).astype(jnp.bfloat16)
    key_width = qkv_weight.shape[3]
    projection = qkv_weight.reshape(model_width, 3 * key_width)
    triple = jnp.dot(
        lax.all_gather(group_normed, "head", axis=0, tiled=True),
        projection,
        preferred_element_type=jnp.float32,
    ).astype(jnp.bfloat16)
    batch_rows = lax.axis_size("head")
    triple = triple.reshape(batch_rows, per_device, 3, key_width)
    query_rows = triple[:, :, 0]
    key_rows = triple[:, :, 1]
    values = triple[:, :, 2]
    query_pos = seq_index * per_device + jnp.arange(per_device, dtype=jnp.int32)
    row_max = jnp.full((batch_rows, per_device), -1e30, jnp.float32)
    key_fragment = lax.all_gather(key_rows, "seq", axis=1, tiled=True)
    value_piece = lax.all_gather(values, "seq", axis=1, tiled=True)
    key_count = key_fragment.shape[1]
    scores = jnp.einsum(
        "tfv,tuv->tfu", query_rows, key_fragment, preferred_element_type=jnp.float32
    ) / math.sqrt(key_width)
    key_pos = jnp.arange(key_count, dtype=jnp.int32)
    allowed = key_pos[None, None, :] <= query_pos[None, :, None]
    new_max = jnp.maximum(row_max, jnp.max(jnp.where(allowed, scores, -1e30), axis=-1))
    exp_scores = jnp.where(
        allowed, jnp.exp(jnp.where(allowed, scores - new_max[:, :, None], 0.0)), 0.0
    )
    row_total = jnp.sum(exp_scores, axis=-1)
    summed = jnp.einsum(
        "vhf,vfy->vhy",
        exp_scores.astype(jnp.bfloat16),
        value_piece,
        preferred_element_type=jnp.float32,
    )
    row_max, row_total, summed = (new_max, row_total, summed)
    attended = (
        (summed / row_total[:, :, None])
        .astype(jnp.bfloat16)
        .reshape(batch_rows, per_device, 1, key_width)
    )
    return (encoded[None], attended)


def solution(mesh):
    placed = (
        P("head", "seq", None),
        P("head", "seq", None),
        P("head", None),
        P("head", None),
        P(),
        P(),
        P("head", None),
        P(None, None, "head", None),
    )
    return jax.shard_map(
        local,
        mesh=mesh,
        in_specs=placed,
        out_specs=(P("head", "seq", None), P(None, "seq", "head", None)),
        check_vma=False,
    )
```

```python
import math

import jax
import jax.numpy as jnp
from jax import lax
from jax.sharding import PartitionSpec as P

BLOCK = 128


highest = lax.Precision.HIGHEST


def passed_along(value, axis, steps):
    count = lax.axis_size(axis)
    first, last = (max(0, -steps), min(count, count - steps))
    return lax.ppermute(value, axis, [(source, source + steps) for source in range(first, last)])


def convolve(padded, conv_weight, length):
    summed = jnp.zeros((length, padded.shape[1]), jnp.float32)
    for offset in range(conv_weight.shape[0]):
        summed = summed + conv_weight[offset] * padded[offset : offset + length].astype(jnp.float32)
    return jax.nn.silu(summed).astype(jnp.bfloat16)


def pieces(values):
    parts, rest = [], values
    for _ in range(3):
        part = lax.reduce_precision(rest, 8, 7)
        parts.append(part.astype(jnp.bfloat16))
        rest = rest - part
    return parts


def head_columns(array, first, own_heads, head_dim, axis):
    return jnp.concatenate(
        [
            lax.dynamic_slice_in_dim(array, first + head * head_dim, head_dim, axis)
            for head in own_heads
        ],
        axis=axis,
    )


def mix(head_inputs, write_vectors, read_vectors, decays):
    blocks, length, heads, head_dim = head_inputs.shape
    later = lax.broadcasted_iota(jnp.int32, (length, length), 0)
    earlier = lax.broadcasted_iota(jnp.int32, (length, length), 1)
    causal = earlier <= later
    cumulative = jnp.einsum(
        "ts,bsh->bht", causal.astype(jnp.float32), decays, precision=highest
    )
    spread = cumulative[:, :, :, None] - cumulative[:, :, None, :]
    factor = jnp.where(causal, jnp.exp(jnp.where(causal, spread, 0.0)), 0.0)
    gram_matrix = jnp.einsum(
        "btn,bsn->bts", read_vectors, write_vectors, preferred_element_type=jnp.float32
    )
    mixed = (factor * gram_matrix[:, None]).astype(jnp.bfloat16)
    output = jnp.einsum("bhts,bshp->bhtp", mixed, head_inputs, preferred_element_type=jnp.float32)
    final_log = cumulative[:, :, -1]
    tail_decay = jnp.exp(final_log[:, :, None] - cumulative)
    weighted = (
        head_inputs.astype(jnp.float32) * tail_decay.transpose(0, 2, 1)[..., None]
    ).astype(jnp.bfloat16)
    fresh = jnp.einsum(
        "bshp,bsn->bhpn", weighted, write_vectors, preferred_element_type=jnp.float32
    )
    state = jnp.zeros_like(fresh[0])
    before = []
    for block in range(blocks):
        before.append(state.astype(jnp.bfloat16))
        state = jnp.exp(final_log[block])[:, None, None] * state + fresh[block]
    carried = jnp.einsum(
        "btn,bhpn->bhtp", read_vectors, jnp.stack(before), preferred_element_type=jnp.float32
    )
    return output + jnp.exp(cumulative)[..., None] * carried


def encode(states, decays, in_weight, conv_weight, norm_gain, out_weight):
    row_count, model_width = states.shape
    head_count = decays.shape[1]
    inner_width = norm_gain.shape[0]
    head_dim = inner_width // head_count
    state_width = (in_weight.shape[1] - 2 * inner_width) // 2
    seq_count, place = lax.axis_size("seq"), lax.axis_index("seq")
    depth_count, depth = lax.axis_size("head"), lax.axis_index("head")
    heads = head_count // seq_count
    shard_heads = head_count // depth_count
    spread_out = shard_heads % seq_count == 0
    if spread_out:
        own_heads = [place + seq_count * k for k in range(heads)]
    else:
        own_heads = [place * heads + k for k in range(heads)]
    weight = jnp.concatenate(
        [
            head_columns(in_weight, 0, own_heads, head_dim, 1),
            head_columns(in_weight, inner_width, own_heads, head_dim, 1),
            in_weight[:, 2 * inner_width :],
        ],
        axis=1,
    )
    weight = lax.all_gather(weight, "head", axis=0, tiled=True)
    if spread_out:
        here = [place + seq_count * k for k in range(shard_heads // seq_count)]
        back = lax.all_gather(
            head_columns(out_weight, 0, here, head_dim, 0), "head", axis=0, tiled=True
        )
    else:
        rows = heads * head_dim
        owner = (place * rows) // out_weight.shape[0]
        slab = lax.dynamic_slice_in_dim(out_weight, place * rows - owner * out_weight.shape[0], rows)
        back = lax.psum(jnp.where(owner == depth, slab, jnp.zeros_like(slab)), "head")
    float_states = states.astype(jnp.float32)
    normed = (
        float_states
        * lax.rsqrt(jnp.mean(float_states * float_states, axis=-1, keepdims=True) + 1e-05)
    ).astype(jnp.bfloat16)
    gathered = lax.all_gather(
        jnp.concatenate([normed, *pieces(decays)], axis=1), "seq", axis=0, tiled=True
    )
    length = gathered.shape[0]
    projected = jnp.dot(
        gathered[:, :model_width], weight, preferred_element_type=jnp.float32
    ).astype(jnp.bfloat16)
    high, middle, low = (
        head_columns(
            gathered[:, model_width + k * head_count : model_width + (k + 1) * head_count],
            0, own_heads, 1, 1,
        ).astype(jnp.float32)
        for k in range(3)
    )
    own_decays = high + (middle + low)
    width = heads * head_dim
    mixer_in = projected[:, width:]
    taps = jnp.concatenate(
        [
            head_columns(conv_weight, 0, own_heads, head_dim, 1),
            conv_weight[:, inner_width:],
        ],
        axis=1,
    )
    padded = jnp.concatenate(
        [jnp.zeros((conv_weight.shape[0] - 1, mixer_in.shape[1]), jnp.bfloat16), mixer_in], axis=0
    )
    convolved = convolve(padded, taps, length)
    blocks = length // BLOCK
    mixed = mix(
        convolved[:, :width].reshape(blocks, BLOCK, heads, head_dim),
        convolved[:, width : width + state_width].reshape(blocks, BLOCK, state_width),
        convolved[:, width + state_width :].reshape(blocks, BLOCK, state_width),
        own_decays.reshape(blocks, BLOCK, heads),
    )
    gate = projected[:, :width].reshape(blocks, BLOCK, heads, head_dim).transpose(0, 2, 1, 3)
    gated = mixed * jax.nn.silu(gate.astype(jnp.float32))
    gain = head_columns(norm_gain, 0, own_heads, head_dim, 0).reshape(heads, 1, head_dim)
    scaled = (
        gated * lax.rsqrt(jnp.mean(gated * gated, axis=-1, keepdims=True) + 1e-05) * gain
    ).astype(jnp.bfloat16)
    flat = scaled.transpose(0, 2, 1, 3).reshape(length, width)
    share = jnp.dot(flat, back, preferred_element_type=jnp.float32).astype(jnp.bfloat16)
    branch = lax.psum_scatter(share, "seq", scatter_dimension=0, tiled=True)
    return (float_states + branch.astype(jnp.float32)).astype(jnp.bfloat16)


def local(
    byte_states, log_decay, group_starts, in_weight, conv_weight, norm_gain, out_weight, qkv_weight
):
    states = byte_states[0]
    starts = group_starts[0]
    row_count, model_width = states.shape
    encoded = encode(states, log_decay[0], in_weight, conv_weight, norm_gain, out_weight)
    seq_count = lax.axis_size("seq")
    seq_index = lax.axis_index("seq")
    groups = starts.shape[0]
    per_device = groups // seq_count
    positions = seq_index * row_count + jnp.arange(row_count, dtype=jnp.int32)
    group_id = jnp.sum((starts[None, :] <= positions[:, None]).astype(jnp.int32), axis=1) - 1
    contract_rows = (((0,), (0,)), ((), ()))
    local_id = group_id - (seq_index - 1) * per_device
    onehot = (local_id[:, None] == jnp.arange(3 * per_device, dtype=jnp.int32)[None, :]).astype(
        jnp.bfloat16
    )
    partial_value = lax.dot_general(
        onehot, encoded, contract_rows, preferred_element_type=jnp.float32
    )
    from_above = passed_along(partial_value[:per_device].astype(jnp.bfloat16), "seq", -1).astype(
        jnp.float32
    )
    from_below = passed_along(
        partial_value[2 * per_device :].astype(jnp.bfloat16), "seq", 1
    ).astype(jnp.float32)
    pooled = partial_value[per_device : 2 * per_device] + from_above + from_below
    group_normed = (
        pooled * lax.rsqrt(jnp.mean(pooled * pooled, axis=-1, keepdims=True) + 1e-05)
    ).astype(jnp.bfloat16)
    key_width = qkv_weight.shape[3]
    projection = qkv_weight.reshape(model_width, 3 * key_width)
    triple = jnp.dot(
        lax.all_gather(group_normed, "head", axis=0, tiled=True),
        projection,
        preferred_element_type=jnp.float32,
    ).astype(jnp.bfloat16)
    batch_rows = lax.axis_size("head")
    triple = triple.reshape(batch_rows, per_device, 3, key_width)
    query_rows = triple[:, :, 0]
    key_rows = triple[:, :, 1]
    values = triple[:, :, 2]
    query_pos = seq_index * per_device + jnp.arange(per_device, dtype=jnp.int32)
    row_max = jnp.full((batch_rows, per_device), -1e30, jnp.float32)
    key_fragment = lax.all_gather(key_rows, "seq", axis=1, tiled=True)
    value_piece = lax.all_gather(values, "seq", axis=1, tiled=True)
    key_count = key_fragment.shape[1]
    scores = jnp.einsum(
        "tfv,tuv->tfu", query_rows, key_fragment, preferred_element_type=jnp.float32
    ) / math.sqrt(key_width)
    key_pos = jnp.arange(key_count, dtype=jnp.int32)
    allowed = key_pos[None, None, :] <= query_pos[None, :, None]
    new_max = jnp.maximum(row_max, jnp.max(jnp.where(allowed, scores, -1e30), axis=-1))
    exp_scores = jnp.where(
        allowed, jnp.exp(jnp.where(allowed, scores - new_max[:, :, None], 0.0)), 0.0
    )
    row_total = jnp.sum(exp_scores, axis=-1)
    summed = jnp.einsum(
        "vhf,vfy->vhy",
        exp_scores.astype(jnp.bfloat16),
        value_piece,
        preferred_element_type=jnp.float32,
    )
    row_max, row_total, summed = (new_max, row_total, summed)
    attended = (
        (summed / row_total[:, :, None])
        .astype(jnp.bfloat16)
        .reshape(batch_rows, per_device, 1, key_width)
    )
    return (encoded[None], attended)


def solution(mesh):
    placed = (
        P("head", "seq", None),
        P("head", "seq", None),
        P("head", None),
        P("head", None),
        P(),
        P(),
        P("head", None),
        P(None, None, "head", None),
    )
    return jax.shard_map(
        local,
        mesh=mesh,
        in_specs=placed,
        out_specs=(P("head", "seq", None), P(None, "seq", "head", None)),
        check_vma=False,
    )
```

```python
import functools
import math

import jax
import jax.numpy as jnp
from jax import lax
from jax.experimental import pallas as pl
from jax.experimental.pallas import tpu as pltpu
from jax.sharding import PartitionSpec as P

BLOCK = 128


highest = lax.Precision.HIGHEST


def passed_along(value, axis, steps):
    count = lax.axis_size(axis)
    first, last = (max(0, -steps), min(count, count - steps))
    return lax.ppermute(value, axis, [(source, source + steps) for source in range(first, last)])


def convolve(padded, conv_weight, length):
    summed = jnp.zeros((length, padded.shape[1]), jnp.float32)
    for offset in range(conv_weight.shape[0]):
        summed = summed + conv_weight[offset] * padded[offset : offset + length].astype(jnp.float32)
    return jax.nn.silu(summed).astype(jnp.bfloat16)


def exchange_kernel(plan, *refs):
    count = len(plan)
    inputs, outputs, semaphores = refs[:count], refs[count : 2 * count], refs[2 * count :]
    barrier = pltpu.get_barrier_semaphore()
    partners = 0
    for axis in sorted({axis for axis, _, _ in plan}):
        size, me = lax.axis_size(axis), lax.axis_index(axis)
        for step in range(1, size):
            pl.semaphore_signal(
                barrier,
                inc=1,
                device_id={axis: lax.rem(me + step, size)},
                device_id_type=pl.DeviceIdType.MESH,
            )
            partners += 1
    pl.semaphore_wait(barrier, partners)
    local_copies, sent, awaited = [], [], []
    for item, (axis, scatter, _) in enumerate(plan):
        source, target = inputs[item], outputs[item]
        send, receive, own = semaphores[3 * item : 3 * item + 3]
        size, me = lax.axis_size(axis), lax.axis_index(axis)
        for step in range(1, size):
            there, origin = lax.rem(me + step, size), lax.rem(me + size - step, size)

            def copy(landing):
                return pltpu.make_async_remote_copy(
                    src_ref=source.at[there] if scatter else source,
                    dst_ref=target.at[landing],
                    send_sem=send.at[step],
                    recv_sem=receive.at[step],
                    device_id={axis: there},
                    device_id_type=pl.DeviceIdType.MESH,
                )

            outgoing = copy(me)
            outgoing.start()
            sent.append(outgoing)
            awaited.append(copy(origin))
        kept = pltpu.make_async_copy(
            source.at[me] if scatter else source, target.at[me], own.at[0]
        )
        kept.start()
        local_copies.append(kept)
    for kept in local_copies:
        kept.wait()
    for arriving in awaited:
        arriving.wait_recv()
    for outgoing in sent:
        outgoing.wait_send()


def exchange(number, *items):
    plan = tuple((axis, scatter, array.shape) for array, axis, scatter in items)
    scratch, shapes = [], []
    for array, axis, scatter in items:
        size = lax.axis_size(axis)
        shapes.append(
            jax.ShapeDtypeStruct(array.shape if scatter else (size, *array.shape), array.dtype)
        )
        scratch += [
            pltpu.SemaphoreType.DMA((size,)),
            pltpu.SemaphoreType.DMA((size,)),
            pltpu.SemaphoreType.DMA((1,)),
        ]
    return pl.pallas_call(
        functools.partial(exchange_kernel, plan),
        out_shape=shapes,
        in_specs=[pl.BlockSpec(memory_space=pltpu.VMEM)] * len(items),
        out_specs=[pl.BlockSpec(memory_space=pltpu.VMEM)] * len(items),
        scratch_shapes=scratch,
        compiler_params=pltpu.CompilerParams(
            collective_id=number, has_side_effects=True, vmem_limit_bytes=32 * 2**20
        ),
    )(*[array for array, _, _ in items])


def pieces(values):
    parts, rest = [], values
    for _ in range(3):
        part = lax.reduce_precision(rest, 8, 7)
        parts.append(part.astype(jnp.bfloat16))
        rest = rest - part
    return parts


def head_columns(array, first, own_heads, head_dim, axis):
    return jnp.concatenate(
        [
            lax.dynamic_slice_in_dim(array, first + head * head_dim, head_dim, axis)
            for head in own_heads
        ],
        axis=axis,
    )


def mix(head_inputs, write_vectors, read_vectors, decays):
    blocks, length, heads, head_dim = head_inputs.shape
    later = lax.broadcasted_iota(jnp.int32, (length, length), 0)
    earlier = lax.broadcasted_iota(jnp.int32, (length, length), 1)
    causal = earlier <= later
    cumulative = jnp.einsum(
        "ts,bsh->bht", causal.astype(jnp.float32), decays, precision=highest
    )
    spread = cumulative[:, :, :, None] - cumulative[:, :, None, :]
    factor = jnp.where(causal, jnp.exp(jnp.where(causal, spread, 0.0)), 0.0)
    gram_matrix = jnp.einsum(
        "btn,bsn->bts", read_vectors, write_vectors, preferred_element_type=jnp.float32
    )
    mixed = (factor * gram_matrix[:, None]).astype(jnp.bfloat16)
    output = jnp.einsum("bhts,bshp->bhtp", mixed, head_inputs, preferred_element_type=jnp.float32)
    final_log = cumulative[:, :, -1]
    tail_decay = jnp.exp(final_log[:, :, None] - cumulative)
    weighted = (
        head_inputs.astype(jnp.float32) * tail_decay.transpose(0, 2, 1)[..., None]
    ).astype(jnp.bfloat16)
    fresh = jnp.einsum(
        "bshp,bsn->bhpn", weighted, write_vectors, preferred_element_type=jnp.float32
    )
    state = jnp.zeros_like(fresh[0])
    before = []
    for block in range(blocks):
        before.append(state.astype(jnp.bfloat16))
        state = jnp.exp(final_log[block])[:, None, None] * state + fresh[block]
    carried = jnp.einsum(
        "btn,bhpn->bhtp", read_vectors, jnp.stack(before), preferred_element_type=jnp.float32
    )
    return output + jnp.exp(cumulative)[..., None] * carried


def encode(states, decays, in_weight, conv_weight, norm_gain, out_weight):
    row_count, model_width = states.shape
    head_count = decays.shape[1]
    inner_width = norm_gain.shape[0]
    head_dim = inner_width // head_count
    state_width = (in_weight.shape[1] - 2 * inner_width) // 2
    seq_count, place = lax.axis_size("seq"), lax.axis_index("seq")
    depth_count, depth = lax.axis_size("head"), lax.axis_index("head")
    heads = head_count // seq_count
    shard_heads = head_count // depth_count
    spread_out = shard_heads % seq_count == 0
    if spread_out:
        own_heads = [place + seq_count * k for k in range(heads)]
    else:
        own_heads = [place * heads + k for k in range(heads)]
    weight = jnp.concatenate(
        [
            head_columns(in_weight, 0, own_heads, head_dim, 1),
            head_columns(in_weight, inner_width, own_heads, head_dim, 1),
            in_weight[:, 2 * inner_width :],
        ],
        axis=1,
    )
    to_gather = [(weight, "head", False)]
    if spread_out:
        here = [place + seq_count * k for k in range(shard_heads // seq_count)]
        to_gather.append((head_columns(out_weight, 0, here, head_dim, 0), "head", False))
    else:
        rows = heads * head_dim
        owner = (place * rows) // out_weight.shape[0]
        slab = lax.dynamic_slice_in_dim(out_weight, place * rows - owner * out_weight.shape[0], rows)
        back = lax.psum(jnp.where(owner == depth, slab, jnp.zeros_like(slab)), "head")
    float_states = states.astype(jnp.float32)
    normed = (
        float_states
        * lax.rsqrt(jnp.mean(float_states * float_states, axis=-1, keepdims=True) + 1e-05)
    ).astype(jnp.bfloat16)
    unused = jnp.zeros((row_count, -3 * head_count % 128), jnp.bfloat16)
    packed = jnp.concatenate([normed, *pieces(decays), unused], axis=1)
    weight, *rest, gathered = exchange(0, *to_gather, (packed, "seq", False))
    weight = weight.reshape(model_width, weight.shape[2])
    if spread_out:
        back = rest[0].reshape(heads * head_dim, model_width)
    gathered = gathered.reshape(seq_count * row_count, packed.shape[1])
    length = gathered.shape[0]
    projected = jnp.dot(
        gathered[:, :model_width], weight, preferred_element_type=jnp.float32
    ).astype(jnp.bfloat16)
    high, middle, low = (
        head_columns(
            gathered[:, model_width + k * head_count : model_width + (k + 1) * head_count],
            0, own_heads, 1, 1,
        ).astype(jnp.float32)
        for k in range(3)
    )
    own_decays = high + (middle + low)
    width = heads * head_dim
    mixer_in = projected[:, width:]
    taps = jnp.concatenate(
        [
            head_columns(conv_weight, 0, own_heads, head_dim, 1),
            conv_weight[:, inner_width:],
        ],
        axis=1,
    )
    padded = jnp.concatenate(
        [jnp.zeros((conv_weight.shape[0] - 1, mixer_in.shape[1]), jnp.bfloat16), mixer_in], axis=0
    )
    convolved = convolve(padded, taps, length)
    blocks = length // BLOCK
    mixed = mix(
        convolved[:, :width].reshape(blocks, BLOCK, heads, head_dim),
        convolved[:, width : width + state_width].reshape(blocks, BLOCK, state_width),
        convolved[:, width + state_width :].reshape(blocks, BLOCK, state_width),
        own_decays.reshape(blocks, BLOCK, heads),
    )
    gate = projected[:, :width].reshape(blocks, BLOCK, heads, head_dim).transpose(0, 2, 1, 3)
    gated = mixed * jax.nn.silu(gate.astype(jnp.float32))
    gain = head_columns(norm_gain, 0, own_heads, head_dim, 0).reshape(heads, 1, head_dim)
    scaled = (
        gated * lax.rsqrt(jnp.mean(gated * gated, axis=-1, keepdims=True) + 1e-05) * gain
    ).astype(jnp.bfloat16)
    flat = scaled.transpose(0, 2, 1, 3).reshape(length, width)
    share = jnp.dot(flat, back, preferred_element_type=jnp.float32).astype(jnp.bfloat16)
    [shares] = exchange(1, (share.reshape(seq_count, row_count, model_width), "seq", True))
    branch = jnp.sum(shares.astype(jnp.float32), axis=0)
    return (float_states + branch).astype(jnp.bfloat16)


def local(
    byte_states, log_decay, group_starts, in_weight, conv_weight, norm_gain, out_weight, qkv_weight
):
    states = byte_states[0]
    starts = group_starts[0]
    row_count, model_width = states.shape
    encoded = encode(states, log_decay[0], in_weight, conv_weight, norm_gain, out_weight)
    seq_count = lax.axis_size("seq")
    seq_index = lax.axis_index("seq")
    groups = starts.shape[0]
    per_device = groups // seq_count
    positions = seq_index * row_count + jnp.arange(row_count, dtype=jnp.int32)
    group_id = jnp.sum((starts[None, :] <= positions[:, None]).astype(jnp.int32), axis=1) - 1
    contract_rows = (((0,), (0,)), ((), ()))
    local_id = group_id - (seq_index - 1) * per_device
    onehot = (local_id[:, None] == jnp.arange(3 * per_device, dtype=jnp.int32)[None, :]).astype(
        jnp.bfloat16
    )
    partial_value = lax.dot_general(
        onehot, encoded, contract_rows, preferred_element_type=jnp.float32
    )
    from_above = passed_along(partial_value[:per_device].astype(jnp.bfloat16), "seq", -1).astype(
        jnp.float32
    )
    from_below = passed_along(
        partial_value[2 * per_device :].astype(jnp.bfloat16), "seq", 1
    ).astype(jnp.float32)
    pooled = partial_value[per_device : 2 * per_device] + from_above + from_below
    group_normed = (
        pooled * lax.rsqrt(jnp.mean(pooled * pooled, axis=-1, keepdims=True) + 1e-05)
    ).astype(jnp.bfloat16)
    key_width = qkv_weight.shape[3]
    projection = qkv_weight.reshape(model_width, 3 * key_width)
    padded_groups = jnp.pad(group_normed, ((0, -per_device % 16), (0, 0)))
    [every_group] = exchange(2, (padded_groups, "head", False))
    triple = jnp.dot(
        every_group[:, :per_device].reshape(-1, model_width),
        projection,
        preferred_element_type=jnp.float32,
    ).astype(jnp.bfloat16)
    batch_rows = lax.axis_size("head")
    triple = triple.reshape(batch_rows, per_device, 3, key_width)
    query_rows = triple[:, :, 0]
    query_pos = seq_index * per_device + jnp.arange(per_device, dtype=jnp.int32)
    row_max = jnp.full((batch_rows, per_device), -1e30, jnp.float32)
    both = triple[:, :, 1:].reshape(batch_rows * per_device, 2 * key_width)
    [both] = exchange(3, (jnp.pad(both, ((0, -both.shape[0] % 16), (0, 0))), "seq", False))
    both = both[:, : batch_rows * per_device].reshape(seq_count, batch_rows, per_device, 2, key_width)
    both = both.transpose(3, 1, 0, 2, 4).reshape(2, batch_rows, groups, key_width)
    key_fragment, value_piece = both[0], both[1]
    key_count = key_fragment.shape[1]
    scores = jnp.einsum(
        "tfv,tuv->tfu", query_rows, key_fragment, preferred_element_type=jnp.float32
    ) / math.sqrt(key_width)
    key_pos = jnp.arange(key_count, dtype=jnp.int32)
    allowed = key_pos[None, None, :] <= query_pos[None, :, None]
    new_max = jnp.maximum(row_max, jnp.max(jnp.where(allowed, scores, -1e30), axis=-1))
    exp_scores = jnp.where(
        allowed, jnp.exp(jnp.where(allowed, scores - new_max[:, :, None], 0.0)), 0.0
    )
    row_total = jnp.sum(exp_scores, axis=-1)
    summed = jnp.einsum(
        "vhf,vfy->vhy",
        exp_scores.astype(jnp.bfloat16),
        value_piece,
        preferred_element_type=jnp.float32,
    )
    row_max, row_total, summed = (new_max, row_total, summed)
    attended = (
        (summed / row_total[:, :, None])
        .astype(jnp.bfloat16)
        .reshape(batch_rows, per_device, 1, key_width)
    )
    return (encoded[None], attended)


def solution(mesh):
    placed = (
        P("head", "seq", None),
        P("head", "seq", None),
        P("head", None),
        P("head", None),
        P(),
        P(),
        P("head", None),
        P(None, None, "head", None),
    )
    return jax.shard_map(
        local,
        mesh=mesh,
        in_specs=placed,
        out_specs=(P("head", "seq", None), P(None, "seq", "head", None)),
        check_vma=False,
    )
```

```python
import functools
import math

import jax
import jax.numpy as jnp
from jax import lax
from jax.experimental import pallas as pl
from jax.experimental.pallas import tpu as pltpu
from jax.sharding import PartitionSpec as P

BLOCK = 128


highest = lax.Precision.HIGHEST


def passed_along(value, axis, steps):
    count = lax.axis_size(axis)
    first, last = (max(0, -steps), min(count, count - steps))
    return lax.ppermute(value, axis, [(source, source + steps) for source in range(first, last)])


def convolve(padded, conv_weight, length):
    summed = jnp.zeros((length, padded.shape[1]), jnp.float32)
    for offset in range(conv_weight.shape[0]):
        summed = summed + conv_weight[offset] * padded[offset : offset + length].astype(jnp.float32)
    return jax.nn.silu(summed).astype(jnp.bfloat16)


def relay_step(axis, source, target, send, receive, step, finish=False):
    size, me = lax.axis_size(axis), lax.axis_index(axis)
    for lane, way in enumerate((1, -1)):
        block = jnp.clip(me - way * step, 0, size - 1)
        exists = (me >= step) if way == 1 else (me + step < size)
        onward = (me + 1 < size) if way == 1 else (me >= 1)
        copy = pltpu.make_async_remote_copy(
            src_ref=source if step == 0 else target.at[block],
            dst_ref=target.at[block],
            send_sem=send.at[lane * size + step],
            recv_sem=receive.at[block],
            device_id={axis: jnp.clip(me + way, 0, size - 1)},
            device_id_type=pl.DeviceIdType.MESH,
        )
        if finish:
            pl.when(exists & onward)(copy.wait_send)
            continue
        if step:
            pl.when(exists)(copy.wait_recv)
        if step < size - 1:
            pl.when(exists & onward)(copy.start)


def pair_sum_kernel(
    share, total, landed, summed, pair_send, pair_receive, far_send, far_receive
):
    size, me = lax.axis_size("seq"), lax.axis_index("seq")
    pairs = size // 2
    pair, side = me // 2, lax.rem(me, 2)
    partner = 2 * pair + 1 - side
    barrier = pltpu.get_barrier_semaphore()
    peers = [partner] + [2 * lax.rem(pair + step, pairs) + side for step in range(1, pairs)]
    for peer in peers:
        pl.semaphore_signal(
            barrier, inc=1, device_id={"seq": peer}, device_id_type=pl.DeviceIdType.MESH
        )
    pl.semaphore_wait(barrier, len(peers))
    order = [*range(1, pairs), 0]
    near = []
    for step in order:
        there = lax.rem(pair + step, pairs)
        copy = pltpu.make_async_remote_copy(
            src_ref=share.at[2 * there + 1 - side],
            dst_ref=landed.at[step],
            send_sem=pair_send.at[step],
            recv_sem=pair_receive.at[step],
            device_id={"seq": partner},
            device_id_type=pl.DeviceIdType.MESH,
        )
        copy.start()
        near.append(copy)
    far = []
    for step, arriving in zip(order, near):
        there = lax.rem(pair + step, pairs)
        arriving.wait_recv()
        both = share[2 * there + side].astype(jnp.float32) + landed[step].astype(jnp.float32)
        if step == 0:
            total[0] = both.astype(jnp.bfloat16)
            continue
        summed[step] = both.astype(jnp.bfloat16)
        copy = pltpu.make_async_remote_copy(
            src_ref=summed.at[step],
            dst_ref=total.at[step],
            send_sem=far_send.at[step],
            recv_sem=far_receive.at[step],
            device_id={"seq": 2 * there + side},
            device_id_type=pl.DeviceIdType.MESH,
        )
        copy.start()
        far.append(copy)
    for copy in far:
        copy.wait_recv()
    for copy in near + far:
        copy.wait_send()


def pair_sums(number, share):
    pairs = share.shape[0] // 2
    block = (pairs, *share.shape[1:])
    return pl.pallas_call(
        pair_sum_kernel,
        out_shape=jax.ShapeDtypeStruct(block, share.dtype),
        in_specs=[pl.BlockSpec(memory_space=pltpu.VMEM)],
        out_specs=pl.BlockSpec(memory_space=pltpu.VMEM),
        scratch_shapes=[pltpu.VMEM(block, share.dtype)] * 2
        + [pltpu.SemaphoreType.DMA((pairs,))] * 4,
        compiler_params=pltpu.CompilerParams(
            collective_id=number, has_side_effects=True, vmem_limit_bytes=40 * 2**20
        ),
    )(share)


def exchange_kernel(plan, *refs):
    count = len(plan)
    inputs, outputs, semaphores = refs[:count], refs[count : 2 * count], refs[2 * count :]
    barrier = pltpu.get_barrier_semaphore()
    partners = 0
    for axis in sorted({axis for axis, _, _ in plan}):
        size, me = lax.axis_size(axis), lax.axis_index(axis)
        for step in range(1, size):
            pl.semaphore_signal(
                barrier,
                inc=1,
                device_id={axis: lax.rem(me + step, size)},
                device_id_type=pl.DeviceIdType.MESH,
            )
            partners += 1
    pl.semaphore_wait(barrier, partners)
    local_copies, sent, awaited, relays = [], [], [], []
    for item, (axis, scatter, relayed) in enumerate(plan):
        source, target = inputs[item], outputs[item]
        send, receive, own = semaphores[3 * item : 3 * item + 3]
        size, me = lax.axis_size(axis), lax.axis_index(axis)
        if relayed:
            relay = functools.partial(relay_step, axis, source, target, send, receive)
            relay(0)
            relays.append((relay, size))
            kept = pltpu.make_async_copy(source, target.at[me], own.at[0])
            kept.start()
            local_copies.append(kept)
            continue
        for step in range(1, size):
            there, origin = lax.rem(me + step, size), lax.rem(me + size - step, size)

            def copy(landing):
                return pltpu.make_async_remote_copy(
                    src_ref=source.at[there] if scatter else source,
                    dst_ref=target.at[landing],
                    send_sem=send.at[step],
                    recv_sem=receive.at[step],
                    device_id={axis: there},
                    device_id_type=pl.DeviceIdType.MESH,
                )

            outgoing = copy(me)
            outgoing.start()
            sent.append(outgoing)
            awaited.append(copy(origin))
        kept = pltpu.make_async_copy(
            source.at[me] if scatter else source, target.at[me], own.at[0]
        )
        kept.start()
        local_copies.append(kept)
    for step in range(1, max([size for _, size in relays], default=0)):
        for relay, size in relays:
            if step < size:
                relay(step)
    for relay, size in relays:
        for step in range(size - 1):
            relay(step, finish=True)
    for kept in local_copies:
        kept.wait()
    for arriving in awaited:
        arriving.wait_recv()
    for outgoing in sent:
        outgoing.wait_send()


def exchange(number, *items):
    plan = tuple((axis, kind == "scatter", kind == "relay") for _, axis, kind in items)
    scratch, shapes = [], []
    for array, axis, kind in items:
        size = lax.axis_size(axis)
        shapes.append(
            jax.ShapeDtypeStruct(
                array.shape if kind == "scatter" else (size, *array.shape), array.dtype
            )
        )
        scratch += [
            pltpu.SemaphoreType.DMA((2 * size,)),
            pltpu.SemaphoreType.DMA((size,)),
            pltpu.SemaphoreType.DMA((1,)),
        ]
    return pl.pallas_call(
        functools.partial(exchange_kernel, plan),
        out_shape=shapes,
        in_specs=[pl.BlockSpec(memory_space=pltpu.VMEM)] * len(items),
        out_specs=[pl.BlockSpec(memory_space=pltpu.VMEM)] * len(items),
        scratch_shapes=scratch,
        compiler_params=pltpu.CompilerParams(
            collective_id=number, has_side_effects=True, vmem_limit_bytes=32 * 2**20
        ),
    )(*[array for array, _, _ in items])


def pieces(values):
    parts, rest = [], values
    for _ in range(3):
        part = lax.reduce_precision(rest, 8, 7)
        parts.append(part.astype(jnp.bfloat16))
        rest = rest - part
    return parts


def head_columns(array, first, own_heads, head_dim, axis):
    return jnp.concatenate(
        [
            lax.dynamic_slice_in_dim(array, first + head * head_dim, head_dim, axis)
            for head in own_heads
        ],
        axis=axis,
    )


def mix(head_inputs, write_vectors, read_vectors, decays):
    blocks, length, heads, head_dim = head_inputs.shape
    later = lax.broadcasted_iota(jnp.int32, (length, length), 0)
    earlier = lax.broadcasted_iota(jnp.int32, (length, length), 1)
    causal = earlier <= later
    cumulative = jnp.einsum(
        "ts,bsh->bht", causal.astype(jnp.float32), decays, precision=highest
    )
    spread = cumulative[:, :, :, None] - cumulative[:, :, None, :]
    factor = jnp.where(causal, jnp.exp(jnp.where(causal, spread, 0.0)), 0.0)
    gram_matrix = jnp.einsum(
        "btn,bsn->bts", read_vectors, write_vectors, preferred_element_type=jnp.float32
    )
    mixed = (factor * gram_matrix[:, None]).astype(jnp.bfloat16)
    output = jnp.einsum("bhts,bshp->bhtp", mixed, head_inputs, preferred_element_type=jnp.float32)
    final_log = cumulative[:, :, -1]
    tail_decay = jnp.exp(final_log[:, :, None] - cumulative)
    weighted = (
        head_inputs.astype(jnp.float32) * tail_decay.transpose(0, 2, 1)[..., None]
    ).astype(jnp.bfloat16)
    fresh = jnp.einsum(
        "bshp,bsn->bhpn", weighted, write_vectors, preferred_element_type=jnp.float32
    )
    state = jnp.zeros_like(fresh[0])
    before = []
    for block in range(blocks):
        before.append(state.astype(jnp.bfloat16))
        state = jnp.exp(final_log[block])[:, None, None] * state + fresh[block]
    carried = jnp.einsum(
        "btn,bhpn->bhtp", read_vectors, jnp.stack(before), preferred_element_type=jnp.float32
    )
    return output + jnp.exp(cumulative)[..., None] * carried


def encode(states, decays, in_weight, conv_weight, norm_gain, out_weight):
    row_count, model_width = states.shape
    head_count = decays.shape[1]
    inner_width = norm_gain.shape[0]
    head_dim = inner_width // head_count
    state_width = (in_weight.shape[1] - 2 * inner_width) // 2
    seq_count, place = lax.axis_size("seq"), lax.axis_index("seq")
    depth_count, depth = lax.axis_size("head"), lax.axis_index("head")
    heads = head_count // seq_count
    shard_heads = head_count // depth_count
    spread_out = shard_heads % seq_count == 0
    if spread_out:
        own_heads = [place + seq_count * k for k in range(heads)]
    else:
        own_heads = [place * heads + k for k in range(heads)]
    weight = jnp.concatenate(
        [
            head_columns(in_weight, 0, own_heads, head_dim, 1),
            head_columns(in_weight, inner_width, own_heads, head_dim, 1),
            in_weight[:, 2 * inner_width :],
        ],
        axis=1,
    )
    to_gather = [(weight, "head", "relay")]
    if spread_out:
        here = [place + seq_count * k for k in range(shard_heads // seq_count)]
        to_gather.append((head_columns(out_weight, 0, here, head_dim, 0), "head", "relay"))
    else:
        rows = heads * head_dim
        owner = (place * rows) // out_weight.shape[0]
        slab = lax.dynamic_slice_in_dim(out_weight, place * rows - owner * out_weight.shape[0], rows)
        back = lax.psum(jnp.where(owner == depth, slab, jnp.zeros_like(slab)), "head")
    float_states = states.astype(jnp.float32)
    normed = (
        float_states
        * lax.rsqrt(jnp.mean(float_states * float_states, axis=-1, keepdims=True) + 1e-05)
    ).astype(jnp.bfloat16)
    unused = jnp.zeros((row_count, -3 * head_count % 128), jnp.bfloat16)
    packed = jnp.concatenate([normed, *pieces(decays), unused], axis=1)
    weight, *rest, gathered = exchange(0, *to_gather, (packed, "seq", "gather"))
    weight = weight.reshape(model_width, weight.shape[2])
    if spread_out:
        back = rest[0].reshape(heads * head_dim, model_width)
    gathered = gathered.reshape(seq_count * row_count, packed.shape[1])
    length = gathered.shape[0]
    projected = jnp.dot(
        gathered[:, :model_width], weight, preferred_element_type=jnp.float32
    ).astype(jnp.bfloat16)
    high, middle, low = (
        head_columns(
            gathered[:, model_width + k * head_count : model_width + (k + 1) * head_count],
            0, own_heads, 1, 1,
        ).astype(jnp.float32)
        for k in range(3)
    )
    own_decays = high + (middle + low)
    width = heads * head_dim
    mixer_in = projected[:, width:]
    taps = jnp.concatenate(
        [
            head_columns(conv_weight, 0, own_heads, head_dim, 1),
            conv_weight[:, inner_width:],
        ],
        axis=1,
    )
    padded = jnp.concatenate(
        [jnp.zeros((conv_weight.shape[0] - 1, mixer_in.shape[1]), jnp.bfloat16), mixer_in], axis=0
    )
    convolved = convolve(padded, taps, length)
    blocks = length // BLOCK
    mixed = mix(
        convolved[:, :width].reshape(blocks, BLOCK, heads, head_dim),
        convolved[:, width : width + state_width].reshape(blocks, BLOCK, state_width),
        convolved[:, width + state_width :].reshape(blocks, BLOCK, state_width),
        own_decays.reshape(blocks, BLOCK, heads),
    )
    gate = projected[:, :width].reshape(blocks, BLOCK, heads, head_dim).transpose(0, 2, 1, 3)
    gated = mixed * jax.nn.silu(gate.astype(jnp.float32))
    gain = head_columns(norm_gain, 0, own_heads, head_dim, 0).reshape(heads, 1, head_dim)
    scaled = (
        gated * lax.rsqrt(jnp.mean(gated * gated, axis=-1, keepdims=True) + 1e-05) * gain
    ).astype(jnp.bfloat16)
    flat = scaled.transpose(0, 2, 1, 3).reshape(length, width)
    share = jnp.dot(flat, back, preferred_element_type=jnp.float32).astype(jnp.bfloat16)
    shares = pair_sums(1, share.reshape(seq_count, row_count, model_width))
    branch = jnp.sum(shares.astype(jnp.float32), axis=0)
    return (float_states + branch).astype(jnp.bfloat16)


def local(
    byte_states, log_decay, group_starts, in_weight, conv_weight, norm_gain, out_weight, qkv_weight
):
    states = byte_states[0]
    starts = group_starts[0]
    row_count, model_width = states.shape
    encoded = encode(states, log_decay[0], in_weight, conv_weight, norm_gain, out_weight)
    seq_count = lax.axis_size("seq")
    seq_index = lax.axis_index("seq")
    groups = starts.shape[0]
    per_device = groups // seq_count
    positions = seq_index * row_count + jnp.arange(row_count, dtype=jnp.int32)
    group_id = jnp.sum((starts[None, :] <= positions[:, None]).astype(jnp.int32), axis=1) - 1
    contract_rows = (((0,), (0,)), ((), ()))
    local_id = group_id - (seq_index - 1) * per_device
    onehot = (local_id[:, None] == jnp.arange(3 * per_device, dtype=jnp.int32)[None, :]).astype(
        jnp.bfloat16
    )
    partial_value = lax.dot_general(
        onehot, encoded, contract_rows, preferred_element_type=jnp.float32
    )
    from_above = passed_along(partial_value[:per_device].astype(jnp.bfloat16), "seq", -1).astype(
        jnp.float32
    )
    from_below = passed_along(
        partial_value[2 * per_device :].astype(jnp.bfloat16), "seq", 1
    ).astype(jnp.float32)
    pooled = partial_value[per_device : 2 * per_device] + from_above + from_below
    group_normed = (
        pooled * lax.rsqrt(jnp.mean(pooled * pooled, axis=-1, keepdims=True) + 1e-05)
    ).astype(jnp.bfloat16)
    key_width = qkv_weight.shape[3]
    projection = qkv_weight.reshape(model_width, 3 * key_width)
    padded_groups = jnp.pad(group_normed, ((0, -per_device % 16), (0, 0)))
    [every_group] = exchange(2, (padded_groups, "head", "gather"))
    triple = jnp.dot(
        every_group[:, :per_device].reshape(-1, model_width),
        projection,
        preferred_element_type=jnp.float32,
    ).astype(jnp.bfloat16)
    batch_rows = lax.axis_size("head")
    triple = triple.reshape(batch_rows, per_device, 3, key_width)
    query_rows = triple[:, :, 0]
    query_pos = seq_index * per_device + jnp.arange(per_device, dtype=jnp.int32)
    row_max = jnp.full((batch_rows, per_device), -1e30, jnp.float32)
    both = triple[:, :, 1:].reshape(batch_rows * per_device, 2 * key_width)
    [both] = exchange(3, (jnp.pad(both, ((0, -both.shape[0] % 16), (0, 0))), "seq", "gather"))
    both = both[:, : batch_rows * per_device].reshape(seq_count, batch_rows, per_device, 2, key_width)
    both = both.transpose(3, 1, 0, 2, 4).reshape(2, batch_rows, groups, key_width)
    key_fragment, value_piece = both[0], both[1]
    key_count = key_fragment.shape[1]
    scores = jnp.einsum(
        "tfv,tuv->tfu", query_rows, key_fragment, preferred_element_type=jnp.float32
    ) / math.sqrt(key_width)
    key_pos = jnp.arange(key_count, dtype=jnp.int32)
    allowed = key_pos[None, None, :] <= query_pos[None, :, None]
    new_max = jnp.maximum(row_max, jnp.max(jnp.where(allowed, scores, -1e30), axis=-1))
    exp_scores = jnp.where(
        allowed, jnp.exp(jnp.where(allowed, scores - new_max[:, :, None], 0.0)), 0.0
    )
    row_total = jnp.sum(exp_scores, axis=-1)
    summed = jnp.einsum(
        "vhf,vfy->vhy",
        exp_scores.astype(jnp.bfloat16),
        value_piece,
        preferred_element_type=jnp.float32,
    )
    row_max, row_total, summed = (new_max, row_total, summed)
    attended = (
        (summed / row_total[:, :, None])
        .astype(jnp.bfloat16)
        .reshape(batch_rows, per_device, 1, key_width)
    )
    return (encoded[None], attended)


def solution(mesh):
    placed = (
        P("head", "seq", None),
        P("head", "seq", None),
        P("head", None),
        P("head", None),
        P(),
        P(),
        P("head", None),
        P(None, None, "head", None),
    )
    return jax.shard_map(
        local,
        mesh=mesh,
        in_specs=placed,
        out_specs=(P("head", "seq", None), P(None, "seq", "head", None)),
        check_vma=False,
    )
```

```python
import functools
import math

import jax
import jax.numpy as jnp
from jax import lax
from jax.experimental import pallas as pl
from jax.experimental.pallas import tpu as pltpu
from jax.sharding import PartitionSpec as P

BLOCK = 128


highest = lax.Precision.HIGHEST


def passed_along(value, axis, steps):
    count = lax.axis_size(axis)
    first, last = (max(0, -steps), min(count, count - steps))
    return lax.ppermute(value, axis, [(source, source + steps) for source in range(first, last)])


def convolve(padded, conv_weight, length):
    summed = jnp.zeros((length, padded.shape[1]), jnp.float32)
    for offset in range(conv_weight.shape[0]):
        summed = summed + conv_weight[offset] * padded[offset : offset + length].astype(jnp.float32)
    return jax.nn.silu(summed).astype(jnp.bfloat16)


def relay_step(axis, source, target, send, receive, step, finish=False):
    size, me = lax.axis_size(axis), lax.axis_index(axis)
    for lane, way in enumerate((1, -1)):
        block = jnp.clip(me - way * step, 0, size - 1)
        exists = (me >= step) if way == 1 else (me + step < size)
        onward = (me + 1 < size) if way == 1 else (me >= 1)
        copy = pltpu.make_async_remote_copy(
            src_ref=source if step == 0 else target.at[block],
            dst_ref=target.at[block],
            send_sem=send.at[lane * size + step],
            recv_sem=receive.at[block],
            device_id={axis: jnp.clip(me + way, 0, size - 1)},
            device_id_type=pl.DeviceIdType.MESH,
        )
        if finish:
            pl.when(exists & onward)(copy.wait_send)
            continue
        if step:
            pl.when(exists)(copy.wait_recv)
        if step < size - 1:
            pl.when(exists & onward)(copy.start)


def pair_sum_kernel(
    share, total, landed, summed, pair_send, pair_receive, far_send, far_receive
):
    size, me = lax.axis_size("seq"), lax.axis_index("seq")
    pairs = size // 2
    pair, side = me // 2, lax.rem(me, 2)
    partner = 2 * pair + 1 - side
    barrier = pltpu.get_barrier_semaphore()
    peers = [partner] + [2 * lax.rem(pair + step, pairs) + side for step in range(1, pairs)]
    for peer in peers:
        pl.semaphore_signal(
            barrier, inc=1, device_id={"seq": peer}, device_id_type=pl.DeviceIdType.MESH
        )
    pl.semaphore_wait(barrier, len(peers))
    order = [*range(1, pairs), 0]
    near = []
    for step in order:
        there = lax.rem(pair + step, pairs)
        copy = pltpu.make_async_remote_copy(
            src_ref=share.at[2 * there + 1 - side],
            dst_ref=landed.at[step],
            send_sem=pair_send.at[step],
            recv_sem=pair_receive.at[step],
            device_id={"seq": partner},
            device_id_type=pl.DeviceIdType.MESH,
        )
        copy.start()
        near.append(copy)
    far = []
    for step, arriving in zip(order, near):
        there = lax.rem(pair + step, pairs)
        arriving.wait_recv()
        both = share[2 * there + side].astype(jnp.float32) + landed[step].astype(jnp.float32)
        if step == 0:
            total[0] = both.astype(jnp.bfloat16)
            continue
        summed[step] = both.astype(jnp.bfloat16)
        copy = pltpu.make_async_remote_copy(
            src_ref=summed.at[step],
            dst_ref=total.at[step],
            send_sem=far_send.at[step],
            recv_sem=far_receive.at[step],
            device_id={"seq": 2 * there + side},
            device_id_type=pl.DeviceIdType.MESH,
        )
        copy.start()
        far.append(copy)
    for copy in far:
        copy.wait_recv()
    for copy in near + far:
        copy.wait_send()


def pair_sums(number, share):
    pairs = share.shape[0] // 2
    block = (pairs, *share.shape[1:])
    return pl.pallas_call(
        pair_sum_kernel,
        out_shape=jax.ShapeDtypeStruct(block, share.dtype),
        in_specs=[pl.BlockSpec(memory_space=pltpu.VMEM)],
        out_specs=pl.BlockSpec(memory_space=pltpu.VMEM),
        scratch_shapes=[pltpu.VMEM(block, share.dtype)] * 2
        + [pltpu.SemaphoreType.DMA((pairs,))] * 4,
        compiler_params=pltpu.CompilerParams(
            collective_id=number, has_side_effects=True, vmem_limit_bytes=40 * 2**20
        ),
    )(share)


def exchange_kernel(plan, *refs):
    count = len(plan)
    inputs, outputs, semaphores = refs[:count], refs[count : 2 * count], refs[2 * count :]
    barrier = pltpu.get_barrier_semaphore()
    partners = 0
    for axis in sorted({axis for axis, _, _ in plan}):
        size, me = lax.axis_size(axis), lax.axis_index(axis)
        for step in range(1, size):
            pl.semaphore_signal(
                barrier,
                inc=1,
                device_id={axis: lax.rem(me + step, size)},
                device_id_type=pl.DeviceIdType.MESH,
            )
            partners += 1
    pl.semaphore_wait(barrier, partners)
    local_copies, sent, awaited, relays = [], [], [], []
    for item, (axis, scatter, relayed) in enumerate(plan):
        source, target = inputs[item], outputs[item]
        send, receive, own = semaphores[3 * item : 3 * item + 3]
        size, me = lax.axis_size(axis), lax.axis_index(axis)
        if relayed:
            relay = functools.partial(relay_step, axis, source, target, send, receive)
            relay(0)
            relays.append((relay, size))
            kept = pltpu.make_async_copy(source, target.at[me], own.at[0])
            kept.start()
            local_copies.append(kept)
            continue
        for step in range(1, size):
            there, origin = lax.rem(me + step, size), lax.rem(me + size - step, size)

            def copy(landing):
                return pltpu.make_async_remote_copy(
                    src_ref=source.at[there] if scatter else source,
                    dst_ref=target.at[landing],
                    send_sem=send.at[step],
                    recv_sem=receive.at[step],
                    device_id={axis: there},
                    device_id_type=pl.DeviceIdType.MESH,
                )

            outgoing = copy(me)
            outgoing.start()
            sent.append(outgoing)
            awaited.append(copy(origin))
        kept = pltpu.make_async_copy(
            source.at[me] if scatter else source, target.at[me], own.at[0]
        )
        kept.start()
        local_copies.append(kept)
    for step in range(1, max([size for _, size in relays], default=0)):
        for relay, size in relays:
            if step < size:
                relay(step)
    for relay, size in relays:
        for step in range(size - 1):
            relay(step, finish=True)
    for kept in local_copies:
        kept.wait()
    for arriving in awaited:
        arriving.wait_recv()
    for outgoing in sent:
        outgoing.wait_send()


def exchange(number, *items):
    plan = tuple((axis, kind == "scatter", kind == "relay") for _, axis, kind in items)
    scratch, shapes = [], []
    for array, axis, kind in items:
        size = lax.axis_size(axis)
        shapes.append(
            jax.ShapeDtypeStruct(
                array.shape if kind == "scatter" else (size, *array.shape), array.dtype
            )
        )
        scratch += [
            pltpu.SemaphoreType.DMA((2 * size,)),
            pltpu.SemaphoreType.DMA((size,)),
            pltpu.SemaphoreType.DMA((1,)),
        ]
    return pl.pallas_call(
        functools.partial(exchange_kernel, plan),
        out_shape=shapes,
        in_specs=[pl.BlockSpec(memory_space=pltpu.VMEM)] * len(items),
        out_specs=[pl.BlockSpec(memory_space=pltpu.VMEM)] * len(items),
        scratch_shapes=scratch,
        compiler_params=pltpu.CompilerParams(
            collective_id=number, has_side_effects=True, vmem_limit_bytes=32 * 2**20
        ),
    )(*[array for array, _, _ in items])


def pieces(values):
    parts, rest = [], values
    for _ in range(3):
        part = lax.reduce_precision(rest, 8, 7)
        parts.append(part.astype(jnp.bfloat16))
        rest = rest - part
    return parts


def head_columns(array, first, own_heads, head_dim, axis):
    return jnp.concatenate(
        [
            lax.dynamic_slice_in_dim(array, first + head * head_dim, head_dim, axis)
            for head in own_heads
        ],
        axis=axis,
    )


def mix_kernel(heads, convolved, gate, down, across, gain, back, share, state):
    length = convolved.shape[0]
    width = gate.shape[1]
    head_dim = width // heads
    state_width = (convolved.shape[1] - width) // 2

    @pl.when(pl.program_id(0) == 0)
    def _():
        state[...] = jnp.zeros_like(state)

    later = lax.broadcasted_iota(jnp.int32, (length, length), 0)
    earlier = lax.broadcasted_iota(jnp.int32, (length, length), 1)
    causal = earlier <= later
    write_vectors = convolved[:, width : width + state_width]
    read_vectors = convolved[:, width + state_width :]
    along = (((1,), (1,)), ((), ()))
    gram_matrix = lax.dot_general(
        read_vectors, write_vectors, along, preferred_element_type=jnp.float32
    )
    done = []
    for head in range(heads):
        columns = slice(head * head_dim, (head + 1) * head_dim)
        at_t, at_s = down[:, head : head + 1], across[0, head : head + 1, :]
        factor = jnp.where(causal, jnp.exp(jnp.where(causal, at_t - at_s, 0.0)), 0.0)
        mixed = (factor * gram_matrix).astype(jnp.bfloat16)
        inputs = convolved[:, columns]
        output = jnp.dot(mixed, inputs, preferred_element_type=jnp.float32)
        before = state[head]
        carried = lax.dot_general(
            read_vectors, before.astype(jnp.bfloat16), along, preferred_element_type=jnp.float32
        )
        output = output + jnp.exp(at_t) * carried
        last = at_t[length - 1 :]
        weighted = (inputs.astype(jnp.float32) * jnp.exp(last - at_t)).astype(jnp.bfloat16)
        fresh = lax.dot_general(
            weighted, write_vectors, (((0,), (0,)), ((), ())), preferred_element_type=jnp.float32
        )
        state[head] = jnp.exp(last) * before + fresh
        own_gate = gate[:, columns].astype(jnp.float32)
        gated = output * (own_gate / (1.0 + jnp.exp(-own_gate)))
        square = jnp.mean(gated * gated, axis=-1, keepdims=True)
        done.append((gated * lax.rsqrt(square + 1e-05) * gain[:, columns]).astype(jnp.bfloat16))
    flat = done[0] if heads == 1 else jnp.concatenate(done, axis=1)
    share[...] = jnp.dot(flat, back[...], preferred_element_type=jnp.float32).astype(jnp.bfloat16)


def mix(convolved, gate, decays, gain, back):
    length, heads = decays.shape
    blocks, width, model_width = length // BLOCK, gate.shape[1], back.shape[1]
    state_width = (convolved.shape[1] - width) // 2
    row = lax.broadcasted_iota(jnp.int32, (BLOCK, BLOCK), 0)
    column = lax.broadcasted_iota(jnp.int32, (BLOCK, BLOCK), 1)
    across = jnp.einsum(
        "ts,bsh->bht",
        (column <= row).astype(jnp.float32),
        decays.reshape(blocks, BLOCK, heads),
        precision=highest,
    )
    down = across.transpose(0, 2, 1).reshape(length, heads)

    def rows(columns):
        return pl.BlockSpec((BLOCK, columns), lambda i: (i, 0))

    return pl.pallas_call(
        functools.partial(mix_kernel, heads),
        grid=(blocks,),
        out_shape=jax.ShapeDtypeStruct((length, model_width), jnp.bfloat16),
        in_specs=[
            rows(convolved.shape[1]),
            rows(width),
            rows(heads),
            pl.BlockSpec((1, heads, BLOCK), lambda i: (i, 0, 0)),
            pl.BlockSpec((1, width), lambda i: (0, 0)),
            pl.BlockSpec((width, model_width), lambda i: (0, 0)),
        ],
        out_specs=rows(model_width),
        scratch_shapes=[pltpu.VMEM((heads, width // heads, state_width), jnp.float32)],
        compiler_params=pltpu.CompilerParams(vmem_limit_bytes=16 * 2**20),
    )(convolved, gate, down, across, gain, back)


def encode(states, decays, in_weight, conv_weight, norm_gain, out_weight):
    row_count, model_width = states.shape
    head_count = decays.shape[1]
    inner_width = norm_gain.shape[0]
    head_dim = inner_width // head_count
    state_width = (in_weight.shape[1] - 2 * inner_width) // 2
    seq_count, place = lax.axis_size("seq"), lax.axis_index("seq")
    depth_count, depth = lax.axis_size("head"), lax.axis_index("head")
    heads = head_count // seq_count
    shard_heads = head_count // depth_count
    spread_out = shard_heads % seq_count == 0
    if spread_out:
        own_heads = [place + seq_count * k for k in range(heads)]
    else:
        own_heads = [place * heads + k for k in range(heads)]
    weight = jnp.concatenate(
        [
            head_columns(in_weight, 0, own_heads, head_dim, 1),
            head_columns(in_weight, inner_width, own_heads, head_dim, 1),
            in_weight[:, 2 * inner_width :],
        ],
        axis=1,
    )
    to_gather = [(weight, "head", "relay")]
    if spread_out:
        here = [place + seq_count * k for k in range(shard_heads // seq_count)]
        to_gather.append((head_columns(out_weight, 0, here, head_dim, 0), "head", "relay"))
    else:
        rows = heads * head_dim
        owner = (place * rows) // out_weight.shape[0]
        slab = lax.dynamic_slice_in_dim(out_weight, place * rows - owner * out_weight.shape[0], rows)
        back = lax.psum(jnp.where(owner == depth, slab, jnp.zeros_like(slab)), "head")
    float_states = states.astype(jnp.float32)
    normed = (
        float_states
        * lax.rsqrt(jnp.mean(float_states * float_states, axis=-1, keepdims=True) + 1e-05)
    ).astype(jnp.bfloat16)
    unused = jnp.zeros((row_count, -3 * head_count % 128), jnp.bfloat16)
    packed = jnp.concatenate([normed, *pieces(decays), unused], axis=1)
    weight, *rest, gathered = exchange(0, *to_gather, (packed, "seq", "gather"))
    weight = weight.reshape(model_width, weight.shape[2])
    if spread_out:
        back = rest[0].reshape(heads * head_dim, model_width)
    gathered = gathered.reshape(seq_count * row_count, packed.shape[1])
    length = gathered.shape[0]
    projected = jnp.dot(
        gathered[:, :model_width], weight, preferred_element_type=jnp.float32
    ).astype(jnp.bfloat16)
    high, middle, low = (
        head_columns(
            gathered[:, model_width + k * head_count : model_width + (k + 1) * head_count],
            0, own_heads, 1, 1,
        ).astype(jnp.float32)
        for k in range(3)
    )
    own_decays = high + (middle + low)
    width = heads * head_dim
    mixer_in = projected[:, width:]
    taps = jnp.concatenate(
        [
            head_columns(conv_weight, 0, own_heads, head_dim, 1),
            conv_weight[:, inner_width:],
        ],
        axis=1,
    )
    padded = jnp.concatenate(
        [jnp.zeros((conv_weight.shape[0] - 1, mixer_in.shape[1]), jnp.bfloat16), mixer_in], axis=0
    )
    convolved = convolve(padded, taps, length)
    gain = head_columns(norm_gain, 0, own_heads, head_dim, 0).reshape(1, width)
    share = mix(convolved, projected[:, :width], own_decays, gain, back)
    shares = pair_sums(1, share.reshape(seq_count, row_count, model_width))
    branch = jnp.sum(shares.astype(jnp.float32), axis=0)
    return (float_states + branch).astype(jnp.bfloat16)


def local(
    byte_states, log_decay, group_starts, in_weight, conv_weight, norm_gain, out_weight, qkv_weight
):
    states = byte_states[0]
    starts = group_starts[0]
    row_count, model_width = states.shape
    encoded = encode(states, log_decay[0], in_weight, conv_weight, norm_gain, out_weight)
    seq_count = lax.axis_size("seq")
    seq_index = lax.axis_index("seq")
    groups = starts.shape[0]
    per_device = groups // seq_count
    positions = seq_index * row_count + jnp.arange(row_count, dtype=jnp.int32)
    group_id = jnp.sum((starts[None, :] <= positions[:, None]).astype(jnp.int32), axis=1) - 1
    contract_rows = (((0,), (0,)), ((), ()))
    local_id = group_id - (seq_index - 1) * per_device
    onehot = (local_id[:, None] == jnp.arange(3 * per_device, dtype=jnp.int32)[None, :]).astype(
        jnp.bfloat16
    )
    partial_value = lax.dot_general(
        onehot, encoded, contract_rows, preferred_element_type=jnp.float32
    )
    from_above = passed_along(partial_value[:per_device].astype(jnp.bfloat16), "seq", -1).astype(
        jnp.float32
    )
    from_below = passed_along(
        partial_value[2 * per_device :].astype(jnp.bfloat16), "seq", 1
    ).astype(jnp.float32)
    pooled = partial_value[per_device : 2 * per_device] + from_above + from_below
    group_normed = (
        pooled * lax.rsqrt(jnp.mean(pooled * pooled, axis=-1, keepdims=True) + 1e-05)
    ).astype(jnp.bfloat16)
    key_width = qkv_weight.shape[3]
    projection = qkv_weight.reshape(model_width, 3 * key_width)
    padded_groups = jnp.pad(group_normed, ((0, -per_device % 16), (0, 0)))
    [every_group] = exchange(2, (padded_groups, "head", "gather"))
    triple = jnp.dot(
        every_group[:, :per_device].reshape(-1, model_width),
        projection,
        preferred_element_type=jnp.float32,
    ).astype(jnp.bfloat16)
    batch_rows = lax.axis_size("head")
    triple = triple.reshape(batch_rows, per_device, 3, key_width)
    query_rows = triple[:, :, 0]
    query_pos = seq_index * per_device + jnp.arange(per_device, dtype=jnp.int32)
    row_max = jnp.full((batch_rows, per_device), -1e30, jnp.float32)
    both = triple[:, :, 1:].reshape(batch_rows * per_device, 2 * key_width)
    [both] = exchange(3, (jnp.pad(both, ((0, -both.shape[0] % 16), (0, 0))), "seq", "gather"))
    both = both[:, : batch_rows * per_device].reshape(seq_count, batch_rows, per_device, 2, key_width)
    both = both.transpose(3, 1, 0, 2, 4).reshape(2, batch_rows, groups, key_width)
    key_fragment, value_piece = both[0], both[1]
    key_count = key_fragment.shape[1]
    scores = jnp.einsum(
        "tfv,tuv->tfu", query_rows, key_fragment, preferred_element_type=jnp.float32
    ) / math.sqrt(key_width)
    key_pos = jnp.arange(key_count, dtype=jnp.int32)
    allowed = key_pos[None, None, :] <= query_pos[None, :, None]
    new_max = jnp.maximum(row_max, jnp.max(jnp.where(allowed, scores, -1e30), axis=-1))
    exp_scores = jnp.where(
        allowed, jnp.exp(jnp.where(allowed, scores - new_max[:, :, None], 0.0)), 0.0
    )
    row_total = jnp.sum(exp_scores, axis=-1)
    summed = jnp.einsum(
        "vhf,vfy->vhy",
        exp_scores.astype(jnp.bfloat16),
        value_piece,
        preferred_element_type=jnp.float32,
    )
    row_max, row_total, summed = (new_max, row_total, summed)
    attended = (
        (summed / row_total[:, :, None])
        .astype(jnp.bfloat16)
        .reshape(batch_rows, per_device, 1, key_width)
    )
    return (encoded[None], attended)


def solution(mesh):
    placed = (
        P("head", "seq", None),
        P("head", "seq", None),
        P("head", None),
        P("head", None),
        P(),
        P(),
        P("head", None),
        P(None, None, "head", None),
    )
    return jax.shard_map(
        local,
        mesh=mesh,
        in_specs=placed,
        out_specs=(P("head", "seq", None), P(None, "seq", "head", None)),
        check_vma=False,
    )
```

```python
import functools
import math

import jax
import jax.numpy as jnp
from jax import lax
from jax.experimental import pallas as pl
from jax.experimental.pallas import tpu as pltpu
from jax.sharding import PartitionSpec as P

BLOCK = 128


highest = lax.Precision.HIGHEST


def passed_along(value, axis, steps):
    count = lax.axis_size(axis)
    first, last = (max(0, -steps), min(count, count - steps))
    return lax.ppermute(value, axis, [(source, source + steps) for source in range(first, last)])


def convolve(padded, conv_weight, length):
    summed = jnp.zeros((length, padded.shape[1]), jnp.float32)
    for offset in range(conv_weight.shape[0]):
        summed = summed + conv_weight[offset] * padded[offset : offset + length].astype(jnp.float32)
    return jax.nn.silu(summed).astype(jnp.bfloat16)


def relay_step(axis, source, target, send, receive, step, finish=False):
    size, me = lax.axis_size(axis), lax.axis_index(axis)
    for lane, way in enumerate((1, -1)):
        block = jnp.clip(me - way * step, 0, size - 1)
        exists = (me >= step) if way == 1 else (me + step < size)
        onward = (me + 1 < size) if way == 1 else (me >= 1)
        copy = pltpu.make_async_remote_copy(
            src_ref=source if step == 0 else target.at[block],
            dst_ref=target.at[block],
            send_sem=send.at[lane * size + step],
            recv_sem=receive.at[block],
            device_id={axis: jnp.clip(me + way, 0, size - 1)},
            device_id_type=pl.DeviceIdType.MESH,
        )
        if finish:
            pl.when(exists & onward)(copy.wait_send)
            continue
        if step:
            pl.when(exists)(copy.wait_recv)
        if step < size - 1:
            pl.when(exists & onward)(copy.start)


def pair_sum_kernel(
    share, total, landed, summed, pair_send, pair_receive, far_send, far_receive
):
    size, me = lax.axis_size("seq"), lax.axis_index("seq")
    pairs = size // 2
    pair, side = me // 2, lax.rem(me, 2)
    partner = 2 * pair + 1 - side
    barrier = pltpu.get_barrier_semaphore()
    peers = [partner] + [2 * lax.rem(pair + step, pairs) + side for step in range(1, pairs)]
    for peer in peers:
        pl.semaphore_signal(
            barrier, inc=1, device_id={"seq": peer}, device_id_type=pl.DeviceIdType.MESH
        )
    pl.semaphore_wait(barrier, len(peers))
    order = [*range(1, pairs), 0]
    near = []
    for step in order:
        there = lax.rem(pair + step, pairs)
        copy = pltpu.make_async_remote_copy(
            src_ref=share.at[2 * there + 1 - side],
            dst_ref=landed.at[step],
            send_sem=pair_send.at[step],
            recv_sem=pair_receive.at[step],
            device_id={"seq": partner},
            device_id_type=pl.DeviceIdType.MESH,
        )
        copy.start()
        near.append(copy)
    far = []
    for step, arriving in zip(order, near):
        there = lax.rem(pair + step, pairs)
        arriving.wait_recv()
        both = share[2 * there + side].astype(jnp.float32) + landed[step].astype(jnp.float32)
        if step == 0:
            total[0] = both.astype(jnp.bfloat16)
            continue
        summed[step] = both.astype(jnp.bfloat16)
        copy = pltpu.make_async_remote_copy(
            src_ref=summed.at[step],
            dst_ref=total.at[step],
            send_sem=far_send.at[step],
            recv_sem=far_receive.at[step],
            device_id={"seq": 2 * there + side},
            device_id_type=pl.DeviceIdType.MESH,
        )
        copy.start()
        far.append(copy)
    for copy in far:
        copy.wait_recv()
    for copy in near + far:
        copy.wait_send()


def pair_sums(number, share):
    pairs = share.shape[0] // 2
    block = (pairs, *share.shape[1:])
    return pl.pallas_call(
        pair_sum_kernel,
        out_shape=jax.ShapeDtypeStruct(block, share.dtype),
        in_specs=[pl.BlockSpec(memory_space=pltpu.VMEM)],
        out_specs=pl.BlockSpec(memory_space=pltpu.VMEM),
        scratch_shapes=[pltpu.VMEM(block, share.dtype)] * 2
        + [pltpu.SemaphoreType.DMA((pairs,))] * 4,
        compiler_params=pltpu.CompilerParams(
            collective_id=number, has_side_effects=True, vmem_limit_bytes=40 * 2**20
        ),
    )(share)


def exchange_kernel(plan, *refs):
    count = len(plan)
    inputs, outputs, semaphores = refs[:count], refs[count : 2 * count], refs[2 * count :]
    barrier = pltpu.get_barrier_semaphore()
    partners = 0
    for axis in sorted({axis for axis, _, _ in plan}):
        size, me = lax.axis_size(axis), lax.axis_index(axis)
        for step in range(1, size):
            pl.semaphore_signal(
                barrier,
                inc=1,
                device_id={axis: lax.rem(me + step, size)},
                device_id_type=pl.DeviceIdType.MESH,
            )
            partners += 1
    pl.semaphore_wait(barrier, partners)
    local_copies, sent, awaited, relays = [], [], [], []
    for item, (axis, scatter, relayed) in enumerate(plan):
        source, target = inputs[item], outputs[item]
        send, receive, own = semaphores[3 * item : 3 * item + 3]
        size, me = lax.axis_size(axis), lax.axis_index(axis)
        if relayed:
            relay = functools.partial(relay_step, axis, source, target, send, receive)
            relay(0)
            relays.append((relay, size))
            kept = pltpu.make_async_copy(source, target.at[me], own.at[0])
            kept.start()
            local_copies.append(kept)
            continue
        for step in range(1, size):
            there, origin = lax.rem(me + step, size), lax.rem(me + size - step, size)

            def copy(landing):
                return pltpu.make_async_remote_copy(
                    src_ref=source.at[there] if scatter else source,
                    dst_ref=target.at[landing],
                    send_sem=send.at[step],
                    recv_sem=receive.at[step],
                    device_id={axis: there},
                    device_id_type=pl.DeviceIdType.MESH,
                )

            outgoing = copy(me)
            outgoing.start()
            sent.append(outgoing)
            awaited.append(copy(origin))
        kept = pltpu.make_async_copy(
            source.at[me] if scatter else source, target.at[me], own.at[0]
        )
        kept.start()
        local_copies.append(kept)
    for step in range(1, max([size for _, size in relays], default=0)):
        for relay, size in relays:
            if step < size:
                relay(step)
    for relay, size in relays:
        for step in range(size - 1):
            relay(step, finish=True)
    for kept in local_copies:
        kept.wait()
    for arriving in awaited:
        arriving.wait_recv()
    for outgoing in sent:
        outgoing.wait_send()


def exchange(number, *items):
    plan = tuple((axis, kind == "scatter", kind == "relay") for _, axis, kind in items)
    scratch, shapes = [], []
    for array, axis, kind in items:
        size = lax.axis_size(axis)
        shapes.append(
            jax.ShapeDtypeStruct(
                array.shape if kind == "scatter" else (size, *array.shape), array.dtype
            )
        )
        scratch += [
            pltpu.SemaphoreType.DMA((2 * size,)),
            pltpu.SemaphoreType.DMA((size,)),
            pltpu.SemaphoreType.DMA((1,)),
        ]
    return pl.pallas_call(
        functools.partial(exchange_kernel, plan),
        out_shape=shapes,
        in_specs=[pl.BlockSpec(memory_space=pltpu.VMEM)] * len(items),
        out_specs=[pl.BlockSpec(memory_space=pltpu.VMEM)] * len(items),
        scratch_shapes=scratch,
        compiler_params=pltpu.CompilerParams(
            collective_id=number, has_side_effects=True, vmem_limit_bytes=32 * 2**20
        ),
    )(*[array for array, _, _ in items])


def pieces(values):
    parts, rest = [], values
    for _ in range(3):
        part = lax.reduce_precision(rest, 8, 7)
        parts.append(part.astype(jnp.bfloat16))
        rest = rest - part
    return parts


def head_columns(array, first, own_heads, head_dim, axis):
    return jnp.concatenate(
        [
            lax.dynamic_slice_in_dim(array, first + head * head_dim, head_dim, axis)
            for head in own_heads
        ],
        axis=axis,
    )


def mix_kernel(heads, convolved, gate, down, across, gain, back, share, state):
    length = convolved.shape[0]
    width = gain.shape[1]
    head_dim = width // heads
    state_width = (convolved.shape[1] - width) // 2

    @pl.when(pl.program_id(0) == 0)
    def _():
        state[...] = jnp.zeros_like(state)

    later = lax.broadcasted_iota(jnp.int32, (length, length), 0)
    earlier = lax.broadcasted_iota(jnp.int32, (length, length), 1)
    causal = earlier <= later
    write_vectors = convolved[:, width : width + state_width]
    read_vectors = convolved[:, width + state_width :]
    along = (((1,), (1,)), ((), ()))
    gram_matrix = lax.dot_general(
        read_vectors, write_vectors, along, preferred_element_type=jnp.float32
    )
    done = []
    for head in range(heads):
        columns = slice(head * head_dim, (head + 1) * head_dim)
        at_t, at_s = down[:, head : head + 1], across[0, head : head + 1, :]
        factor = jnp.where(causal, jnp.exp(jnp.where(causal, at_t - at_s, 0.0)), 0.0)
        mixed = (factor * gram_matrix).astype(jnp.bfloat16)
        inputs = convolved[:, columns]
        output = jnp.dot(mixed, inputs, preferred_element_type=jnp.float32)
        before = state[head]
        carried = lax.dot_general(
            read_vectors, before.astype(jnp.bfloat16), along, preferred_element_type=jnp.float32
        )
        output = output + jnp.exp(at_t) * carried
        last = at_t[length - 1 :]
        weighted = (inputs.astype(jnp.float32) * jnp.exp(last - at_t)).astype(jnp.bfloat16)
        fresh = lax.dot_general(
            weighted, write_vectors, (((0,), (0,)), ((), ())), preferred_element_type=jnp.float32
        )
        state[head] = jnp.exp(last) * before + fresh
        own_gate = gate[:, columns].astype(jnp.float32)
        gated = output * (own_gate / (1.0 + jnp.exp(-own_gate)))
        square = jnp.mean(gated * gated, axis=-1, keepdims=True)
        done.append((gated * lax.rsqrt(square + 1e-05) * gain[:, columns]).astype(jnp.bfloat16))
    flat = done[0] if heads == 1 else jnp.concatenate(done, axis=1)
    share[...] = jnp.dot(flat, back[...], preferred_element_type=jnp.float32).astype(jnp.bfloat16)


def mix(convolved, gate, decays, gain, back):
    length, heads = decays.shape
    blocks, width, model_width = length // BLOCK, gain.shape[1], back.shape[1]
    state_width = (convolved.shape[1] - width) // 2
    row = lax.broadcasted_iota(jnp.int32, (BLOCK, BLOCK), 0)
    column = lax.broadcasted_iota(jnp.int32, (BLOCK, BLOCK), 1)
    across = jnp.einsum(
        "ts,bsh->bht",
        (column <= row).astype(jnp.float32),
        decays.reshape(blocks, BLOCK, heads),
        precision=highest,
    )
    down = across.transpose(0, 2, 1).reshape(length, heads)

    def rows(columns):
        return pl.BlockSpec((BLOCK, columns), lambda i: (i, 0))

    return pl.pallas_call(
        functools.partial(mix_kernel, heads),
        grid=(blocks,),
        out_shape=jax.ShapeDtypeStruct((length, model_width), jnp.bfloat16),
        in_specs=[
            rows(convolved.shape[1]),
            rows(gate.shape[1]),
            rows(heads),
            pl.BlockSpec((1, heads, BLOCK), lambda i: (i, 0, 0)),
            pl.BlockSpec((1, width), lambda i: (0, 0)),
            pl.BlockSpec((width, model_width), lambda i: (0, 0)),
        ],
        out_specs=rows(model_width),
        scratch_shapes=[pltpu.VMEM((heads, width // heads, state_width), jnp.float32)],
        compiler_params=pltpu.CompilerParams(vmem_limit_bytes=16 * 2**20),
    )(convolved, gate, down, across, gain, back)


def encode(states, decays, in_weight, conv_weight, norm_gain, out_weight):
    row_count, model_width = states.shape
    head_count = decays.shape[1]
    inner_width = norm_gain.shape[0]
    head_dim = inner_width // head_count
    state_width = (in_weight.shape[1] - 2 * inner_width) // 2
    seq_count, place = lax.axis_size("seq"), lax.axis_index("seq")
    depth_count, depth = lax.axis_size("head"), lax.axis_index("head")
    heads = head_count // seq_count
    shard_heads = head_count // depth_count
    spread_out = shard_heads % seq_count == 0
    if spread_out:
        own_heads = [place + seq_count * k for k in range(heads)]
    else:
        own_heads = [place * heads + k for k in range(heads)]
    weight = jnp.concatenate(
        [
            head_columns(in_weight, 0, own_heads, head_dim, 1),
            head_columns(in_weight, inner_width, own_heads, head_dim, 1),
            in_weight[:, 2 * inner_width :],
        ],
        axis=1,
    )
    to_gather = [(weight, "head", "relay")]
    if spread_out:
        here = [place + seq_count * k for k in range(shard_heads // seq_count)]
        to_gather.append((head_columns(out_weight, 0, here, head_dim, 0), "head", "relay"))
    else:
        rows = heads * head_dim
        owner = (place * rows) // out_weight.shape[0]
        slab = lax.dynamic_slice_in_dim(out_weight, place * rows - owner * out_weight.shape[0], rows)
        back = lax.psum(jnp.where(owner == depth, slab, jnp.zeros_like(slab)), "head")
    float_states = states.astype(jnp.float32)
    normed = (
        float_states
        * lax.rsqrt(jnp.mean(float_states * float_states, axis=-1, keepdims=True) + 1e-05)
    ).astype(jnp.bfloat16)
    unused = jnp.zeros((row_count, -3 * head_count % 128), jnp.bfloat16)
    packed = jnp.concatenate([normed, *pieces(decays), unused], axis=1)
    weight, *rest, gathered = exchange(0, *to_gather, (packed, "seq", "gather"))
    weight = weight.reshape(model_width, weight.shape[2])
    if spread_out:
        back = rest[0].reshape(heads * head_dim, model_width)
    gathered = gathered.reshape(seq_count * row_count, packed.shape[1])
    length = gathered.shape[0]
    projected = jnp.dot(
        gathered[:, :model_width], weight, preferred_element_type=jnp.float32
    ).astype(jnp.bfloat16)
    high, middle, low = (
        head_columns(
            gathered[:, model_width + k * head_count : model_width + (k + 1) * head_count],
            0, own_heads, 1, 1,
        ).astype(jnp.float32)
        for k in range(3)
    )
    own_decays = high + (middle + low)
    width = heads * head_dim
    mixer_in = projected[:, width:]
    taps = jnp.concatenate(
        [
            head_columns(conv_weight, 0, own_heads, head_dim, 1),
            conv_weight[:, inner_width:],
        ],
        axis=1,
    )
    padded = jnp.concatenate(
        [jnp.zeros((conv_weight.shape[0] - 1, mixer_in.shape[1]), jnp.bfloat16), mixer_in], axis=0
    )
    convolved = convolve(padded, taps, length)
    gain = head_columns(norm_gain, 0, own_heads, head_dim, 0).reshape(1, width)
    share = mix(convolved, projected, own_decays, gain, back)
    shares = pair_sums(1, share.reshape(seq_count, row_count, model_width))
    branch = jnp.sum(shares.astype(jnp.float32), axis=0)
    return (float_states + branch).astype(jnp.bfloat16)


def local(
    byte_states, log_decay, group_starts, in_weight, conv_weight, norm_gain, out_weight, qkv_weight
):
    states = byte_states[0]
    starts = group_starts[0]
    row_count, model_width = states.shape
    encoded = encode(states, log_decay[0], in_weight, conv_weight, norm_gain, out_weight)
    seq_count = lax.axis_size("seq")
    seq_index = lax.axis_index("seq")
    groups = starts.shape[0]
    per_device = groups // seq_count
    positions = seq_index * row_count + jnp.arange(row_count, dtype=jnp.int32)
    group_id = jnp.sum((starts[None, :] <= positions[:, None]).astype(jnp.int32), axis=1) - 1
    contract_rows = (((0,), (0,)), ((), ()))
    local_id = group_id - (seq_index - 1) * per_device
    onehot = (local_id[:, None] == jnp.arange(3 * per_device, dtype=jnp.int32)[None, :]).astype(
        jnp.bfloat16
    )
    partial_value = lax.dot_general(
        onehot, encoded, contract_rows, preferred_element_type=jnp.float32
    )
    from_above = passed_along(partial_value[:per_device].astype(jnp.bfloat16), "seq", -1).astype(
        jnp.float32
    )
    from_below = passed_along(
        partial_value[2 * per_device :].astype(jnp.bfloat16), "seq", 1
    ).astype(jnp.float32)
    pooled = partial_value[per_device : 2 * per_device] + from_above + from_below
    group_normed = (
        pooled * lax.rsqrt(jnp.mean(pooled * pooled, axis=-1, keepdims=True) + 1e-05)
    ).astype(jnp.bfloat16)
    key_width = qkv_weight.shape[3]
    projection = qkv_weight.reshape(model_width, 3 * key_width)
    padded_groups = jnp.pad(group_normed, ((0, -per_device % 16), (0, 0)))
    [every_group] = exchange(2, (padded_groups, "head", "gather"))
    triple = jnp.dot(
        every_group[:, :per_device].reshape(-1, model_width),
        projection,
        preferred_element_type=jnp.float32,
    ).astype(jnp.bfloat16)
    batch_rows = lax.axis_size("head")
    triple = triple.reshape(batch_rows, per_device, 3, key_width)
    query_rows = triple[:, :, 0]
    query_pos = seq_index * per_device + jnp.arange(per_device, dtype=jnp.int32)
    row_max = jnp.full((batch_rows, per_device), -1e30, jnp.float32)
    both = triple[:, :, 1:].reshape(batch_rows * per_device, 2 * key_width)
    [both] = exchange(3, (jnp.pad(both, ((0, -both.shape[0] % 16), (0, 0))), "seq", "gather"))
    both = both[:, : batch_rows * per_device].reshape(seq_count, batch_rows, per_device, 2, key_width)
    both = both.transpose(3, 1, 0, 2, 4).reshape(2, batch_rows, groups, key_width)
    key_fragment, value_piece = both[0], both[1]
    key_count = key_fragment.shape[1]
    scores = jnp.einsum(
        "tfv,tuv->tfu", query_rows, key_fragment, preferred_element_type=jnp.float32
    ) / math.sqrt(key_width)
    key_pos = jnp.arange(key_count, dtype=jnp.int32)
    allowed = key_pos[None, None, :] <= query_pos[None, :, None]
    new_max = jnp.maximum(row_max, jnp.max(jnp.where(allowed, scores, -1e30), axis=-1))
    exp_scores = jnp.where(
        allowed, jnp.exp(jnp.where(allowed, scores - new_max[:, :, None], 0.0)), 0.0
    )
    row_total = jnp.sum(exp_scores, axis=-1)
    summed = jnp.einsum(
        "vhf,vfy->vhy",
        exp_scores.astype(jnp.bfloat16),
        value_piece,
        preferred_element_type=jnp.float32,
    )
    row_max, row_total, summed = (new_max, row_total, summed)
    attended = (
        (summed / row_total[:, :, None])
        .astype(jnp.bfloat16)
        .reshape(batch_rows, per_device, 1, key_width)
    )
    return (encoded[None], attended)


def solution(mesh):
    placed = (
        P("head", "seq", None),
        P("head", "seq", None),
        P("head", None),
        P("head", None),
        P(),
        P(),
        P("head", None),
        P(None, None, "head", None),
    )
    return jax.shard_map(
        local,
        mesh=mesh,
        in_specs=placed,
        out_specs=(P("head", "seq", None), P(None, "seq", "head", None)),
        check_vma=False,
    )
```
